32 devices in a mesh: groups: 2 (over y), space: 4 (over z), date: 4 (over x, core).
Axes of the slice: x: 2, y: 2, z: 4, core: 2. Of those that a mesh axis runs over, the one named last changes fastest.
Arguments:
- features: bfloat16 [64, 256, 768], P('date', ('groups', 'space')), parts along dimension 1, may hold values from -6 to 6
- grad_out: bfloat16 [64, 256, 768], P('date', ('groups', 'space')), parts along dimension 1, may hold values from -6 to 6
- w_qkv: bfloat16 [768, 2304], replicated, may hold values from -2 to 2
- w_out: bfloat16 [768, 768], replicated, may hold values from -0.21875 to 0.21875
- valid_dates: int32 [64, 256], P(None, ('groups', 'space', 'date')), parts along dimension 1, may hold values 0 or 1
Outputs:
- grad_in: bfloat16 [64, 256, 768], P('date', ('groups', 'space')), parts along dimension 1
- weight_grad: float32 [1536, 3072], P(('groups', 'space', 'date')), parts along dimension 0
The draws below stay inside these ranges and needn't reach their ends.
There are 2 independent parts, one for each index of `groups`. The reference program is written for one: setup_inputs(seed, part) draws one part's arguments, and reference() takes and returns one part's arrays. A program takes and returns all parts, laid end to end along the dimension named above; an argument that names none is the same for every part. Nothing has to cross between parts.
All inputs are finite; a program needn't handle non-finite values. No bound on the sum of `valid_dates` on one device may be relied on, other than what follows from the above.
Results may differ from the reference program's by a relative error of at most 0.009.
Values may be sent and summed in bfloat16 or wider, within the bound.
A program may use at most 128 MiB of HBM per device.

```python
import jax
import jax.numpy as jnp
from jax import lax

D = 768
H = 12
HD = 64
DATES = 64
PATCHES = 128


def draw_w_qkv(key, part):
    key = jax.random.fold_in(key, 7)
    first = jax.random.fold_in(key, 0)
    base = jax.random.normal(first, (D, 3 * D), jnp.float32) * D ** (-0.5)
    base = jnp.clip(base, -6.0 * D ** (-0.5), 6.0 * D ** (-0.5))
    return jnp.clip(base, -2.0, 2.0).astype(jnp.bfloat16)


def with_ends(array, key, smallest, high):
    spot = [jax.random.randint(jax.random.fold_in(key, axis), (), 0, length) for axis, length in enumerate(array.shape)]
    main_axis = array.shape.index(max(array.shape))
    next_to = spot[:main_axis] + [(spot[main_axis] + 1) % array.shape[main_axis]] + spot[main_axis + 1:]
    return array.at[tuple(spot)].set(smallest).at[tuple(next_to)].set(high)


def with_spikes(result, own_key, source, target, parts, factor):
    owner, partner = [(jnp.arange(result.shape[dim]) // (result.shape[dim] // parts)).reshape([-1 if axis == dim else 1 for axis in range(result.ndim)]) for dim in (source, target)]
    chosen = jax.random.permutation(own_key, parts)[partner]
    strong = (owner == chosen) | (owner == (partner + parts // 2) % parts)
    return jnp.where(strong, factor * result, result)


def block_levels(own_key, dims, cuts, low, top_value):
    gain, own = 1.0, jax.random.fold_in(own_key, 6)
    for position, parts in cuts:
        draws = jnp.exp(jax.random.uniform(jax.random.fold_in(own, position), (parts,), jnp.float32, low / len(cuts), top_value / len(cuts)))
        gain = gain * jnp.repeat(draws, dims[position] // parts).reshape([-1 if axis == position else 1 for axis in range(len(dims))])
    return gain


def noise(own_key, shape, spread, bound, cuts=(), kind=jnp.bfloat16):
    gain = block_levels(own_key, shape, cuts, -0.22, 0.18) if cuts else 1.0
    array = jax.random.normal(own_key, shape, jnp.float32) * spread * gain
    return jnp.minimum(jnp.maximum(array, -bound), bound).astype(kind)


def noise_with(key, shape, scale, limit, shards, heavy, dtype=jnp.bfloat16):
    array = scale * jax.random.normal(key, shape, jnp.float32)
    if shards:
        array = array * block_levels(key, shape, shards, -0.22, 0.18)
    return jnp.clip(with_spikes(array, jax.random.fold_in(key, 3), *heavy), -limit, limit).astype(dtype)


def setup_inputs(seed: int = 0, part: int = 0) -> dict:
    arg_keys = jax.random.split(jax.random.key(seed), 6)
    part_keys = jax.random.split(jax.random.fold_in(arg_keys[5], part), 6)
    features = noise_with(part_keys[0], (DATES, PATCHES, D), 1.0, 6.0, ((0, 4), (1, 4)), (1, 2, 4, 2.0))
    grad_out = noise(part_keys[1], (DATES, PATCHES, D), 1.0, 6.0, ((0, 4), (1, 4)))
    w_qkv = draw_w_qkv(jax.random.fold_in(arg_keys[5], 71), part)
    w_out = noise(arg_keys[3], (D, D), D ** -0.5, 0.21875)
    valid_dates = with_ends((jax.random.randint(part_keys[4], (DATES, PATCHES), 0, 4) < 3).astype(jnp.int32), jax.random.fold_in(part_keys[4], 1), 0, 1)
    return {"features": features, "grad_out": grad_out, "w_qkv": w_qkv, "w_out": w_out, "valid_dates": valid_dates}


epsilon = 1e-05

def normalize(features):
    flat = features.astype(jnp.float32)
    average = lax.optimization_barrier(jnp.mean(flat, axis=-1, keepdims=True))
    centred = flat - average
    variance = lax.optimization_barrier(jnp.mean(centred * centred, axis=-1, keepdims=True))
    inv_std = lax.rsqrt(variance + epsilon)
    return (centred * inv_std, inv_std)

def attend(query, keys, values, d_attn, valid_dates):
    dates = query.shape[0]
    scale = 1.0 / query.shape[-1] ** 0.5
    scores = jnp.einsum('tphd,uphd->phtu', query.astype(jnp.float32), keys.astype(jnp.float32)) * scale
    diagonal = jnp.arange(dates)[:, None] == jnp.arange(dates)[None, :]
    keep = (valid_dates.T[:, None, None, :] == 1) | diagonal[None, None]
    scores = jnp.where(keep, scores, -1e+30)
    highest = lax.optimization_barrier(jnp.max(scores, axis=-1, keepdims=True))
    expon = jnp.where(keep, jnp.exp(scores - highest), 0.0)
    prob = expon / lax.optimization_barrier(jnp.sum(expon, axis=-1, keepdims=True))
    prob_b = prob.astype(jnp.bfloat16)
    attn = jnp.einsum('phtu,uphd->tphd', prob_b.astype(jnp.float32), values.astype(jnp.float32)).astype(jnp.bfloat16)
    d_prob = jnp.einsum('tphd,uphd->phtu', d_attn.astype(jnp.float32), values.astype(jnp.float32))
    delta = lax.optimization_barrier(jnp.sum(prob * d_prob, axis=-1, keepdims=True))
    d_score = (prob * (d_prob - delta) * scale).astype(jnp.bfloat16).astype(jnp.float32)
    d_query = jnp.einsum('phtu,uphd->tphd', d_score, keys.astype(jnp.float32)).astype(jnp.bfloat16)
    d_key = jnp.einsum('phtu,tphd->uphd', d_score, query.astype(jnp.float32)).astype(jnp.bfloat16)
    d_value = jnp.einsum('phtu,tphd->uphd', prob_b.astype(jnp.float32), d_attn.astype(jnp.float32)).astype(jnp.bfloat16)
    return (attn, d_query, d_key, d_value)

def reference(features, grad_out, w_qkv, w_out, valid_dates):
    dates, patches, width = features.shape
    rows = dates * patches
    normed, inv_std = normalize(features)
    normed_b = normed.astype(jnp.bfloat16).reshape(rows, width)
    qkv = jnp.dot(normed_b, w_qkv, preferred_element_type=jnp.float32).astype(jnp.bfloat16)
    qkv = qkv.reshape(dates, patches, 3, H, HD)
    grad_rows = grad_out.reshape(rows, width)
    d_attn = jnp.dot(grad_rows, w_out.T, preferred_element_type=jnp.float32).astype(jnp.bfloat16)
    d_attn = d_attn.reshape(dates, patches, H, HD)
    attn, d_query, d_key, d_value = attend(qkv[:, :, 0], qkv[:, :, 1], qkv[:, :, 2], d_attn, valid_dates)
    d_qkv = jnp.stack([d_query, d_key, d_value], axis=2).reshape(rows, 3 * width)
    d_normed = jnp.dot(d_qkv, w_qkv.T, preferred_element_type=jnp.float32).reshape(dates, patches, width)
    first = lax.optimization_barrier(jnp.mean(d_normed, axis=-1, keepdims=True))
    second = lax.optimization_barrier(jnp.mean(d_normed * normed, axis=-1, keepdims=True))
    grad_in = (grad_out.astype(jnp.float32) + inv_std * (d_normed - first - normed * second)).astype(jnp.bfloat16)
    attn_rows = attn.reshape(rows, width)
    weight_grad = jnp.concatenate([jnp.dot(normed_b.T, d_qkv, preferred_element_type=jnp.float32), jnp.dot(attn_rows.T, grad_rows, preferred_element_type=jnp.float32)], axis=1)
    return (grad_in, weight_grad)
```

```python
import jax
import jax.numpy as jnp
from jax import lax
from jax.experimental import pallas as pl
from jax.experimental.pallas import tpu as pltpu
from jax.sharding import PartitionSpec as P

HD = 64
epsilon = 1e-05
F32 = jnp.float32
BF16 = jnp.bfloat16
NT = (((1,), (1,)), ((), ()))
TN = (((0,), (0,)), ((), ()))
ROWS = 128


def stats(rows):
    flat = rows.astype(F32)
    centred = flat - jnp.mean(flat, axis=-1, keepdims=True)
    variance = jnp.mean(centred * centred, axis=-1, keepdims=True)
    inv_std = lax.rsqrt(variance + epsilon)
    return centred * inv_std, inv_std


def group_rows(ref, i):
    dates, width = ref.shape[1:]
    n = ROWS // dates
    return ref[pl.ds(i * n, n)].reshape(ROWS, width)


def project(i, f_ref, g_ref, wq_ref, wo_ref, nbt, qkv, da):
    normed, _ = stats(group_rows(f_ref, i))
    nb = normed.astype(BF16)
    at = pl.ds(pl.multiple_of(i * ROWS, ROWS), ROWS)
    nbt[:, at] = nb.T
    qkv[at, :] = jnp.dot(nb, wq_ref[...], preferred_element_type=F32).astype(BF16)
    da[at, :] = lax.dot_general(
        group_rows(g_ref, i), wo_ref[...], NT, preferred_element_type=F32
    ).astype(BF16)


def attend(i, dates, vd_ref, qkv, da, att, dqkv):
    width = da.shape[1]
    scale = 1.0 / HD**0.5
    at = pl.ds(pl.multiple_of(i * ROWS, ROWS), ROWS)
    row = lax.broadcasted_iota(jnp.int32, (ROWS, ROWS), 0)
    col = lax.broadcasted_iota(jnp.int32, (ROWS, ROWS), 1)
    keep = ((row // dates) == (col // dates)) & ((vd_ref[i] == 1) | (row == col))
    bias = jnp.where(keep, 0.0, -1e30).astype(F32)
    bias = jnp.concatenate([bias, bias], axis=0)
    lane = lax.broadcasted_iota(jnp.int32, (1, 2 * HD), 1)
    first = jnp.where(lane < HD, 1.0, 0.0).astype(BF16)
    second = jnp.where(lane < HD, 0.0, 1.0).astype(BF16)

    def stack(a):
        return jnp.concatenate([a * first, a * second], axis=0)

    def side(a):
        return jnp.concatenate([a[:ROWS], a[ROWS:]], axis=1)

    for c in range(0, width, 2 * HD):
        q = stack(qkv[at, c : c + 2 * HD])
        k = qkv[at, width + c : width + c + 2 * HD]
        v = qkv[at, 2 * width + c : 2 * width + c + 2 * HD]
        d = stack(da[at, c : c + 2 * HD])
        s = lax.dot_general(q, k, NT, preferred_element_type=F32) * scale + bias
        e = jnp.exp(s - jnp.max(s, axis=-1, keepdims=True))
        prob = e / jnp.sum(e, axis=-1, keepdims=True)
        prob_b = prob.astype(BF16)
        o = jnp.dot(side(prob_b), stack(v), preferred_element_type=F32).astype(BF16)
        att[c : c + 2 * HD, at] = o.T
        dp = lax.dot_general(d, v, NT, preferred_element_type=F32)
        delta = jnp.sum(prob * dp, axis=-1, keepdims=True)
        ds = (prob * (dp - delta) * scale).astype(BF16)
        dqkv[at, c : c + 2 * HD] = jnp.dot(
            side(ds), stack(k), preferred_element_type=F32
        ).astype(BF16)
        dqkv[at, width + c : width + c + 2 * HD] = lax.dot_general(
            ds, q, TN, preferred_element_type=F32
        ).astype(BF16)
        dqkv[at, 2 * width + c : 2 * width + c + 2 * HD] = lax.dot_general(
            prob_b, d, TN, preferred_element_type=F32
        ).astype(BF16)


def norm_backward(i, f_ref, g_ref, wq_ref, dqkv):
    at = pl.ds(pl.multiple_of(i * ROWS, ROWS), ROWS)
    dn = lax.dot_general(dqkv[at, :], wq_ref[...], NT, preferred_element_type=F32)
    normed, inv_std = stats(group_rows(f_ref, i))
    first = jnp.mean(dn, axis=-1, keepdims=True)
    second = jnp.mean(dn * normed, axis=-1, keepdims=True)
    return (group_rows(g_ref, i).astype(F32) + inv_std * (dn - first - normed * second)).astype(
        BF16
    )


def compute_kernel(f_ref, g_ref, wq_ref, wo_ref, vd_ref, gi_ref, wg_ref, nbt, qkv, da, att, dqkv):
    patches, dates, width = f_ref.shape
    groups = patches * dates // ROWS
    n = ROWS // dates

    @pl.loop(0, groups)
    def _(i):
        project(i, f_ref, g_ref, wq_ref, wo_ref, nbt, qkv, da)
        attend(i, dates, vd_ref, qkv, da, att, dqkv)
        gi_ref[pl.ds(i * n, n)] = norm_backward(i, f_ref, g_ref, wq_ref, dqkv).reshape(
            n, dates, width
        )

    tile = 256

    @pl.loop(0, 3 * width // tile)
    def _(j):
        at = pl.ds(pl.multiple_of(j * tile, tile), tile)
        wg_ref[:, at] = jnp.dot(nbt[...], dqkv[:, at], preferred_element_type=F32).astype(BF16)

    for j in range(0, width, tile):
        g = g_ref[:, :, j : j + tile].reshape(patches * dates, tile)
        wg_ref[:, 3 * width + j : 3 * width + j + tile] = jnp.dot(
            att[...], g, preferred_element_type=F32
        ).astype(BF16)


def local(features, grad_out, w_qkv, w_out, valid_dates):
    width = features.shape[-1]
    dates, patches = valid_dates.shape
    tokens = dates * patches
    f = lax.all_to_all(features.transpose(1, 0, 2), "date", split_axis=0, concat_axis=1, tiled=True)
    g = lax.all_to_all(grad_out.transpose(1, 0, 2), "date", split_axis=0, concat_axis=1, tiled=True)
    vd = valid_dates.T.reshape(tokens // ROWS, 1, ROWS)
    vmem = pl.BlockSpec(memory_space=pltpu.VMEM)
    gi, wg = pl.pallas_call(
        compute_kernel,
        out_shape=(
            jax.ShapeDtypeStruct((patches, dates, width), BF16),
            jax.ShapeDtypeStruct((width, 4 * width), BF16),
        ),
        in_specs=[vmem] * 5,
        out_specs=(vmem, vmem),
        scratch_shapes=[
            pltpu.VMEM((width, tokens), BF16),
            pltpu.VMEM((tokens, 3 * width), BF16),
            pltpu.VMEM((tokens, width), BF16),
            pltpu.VMEM((width, tokens), BF16),
            pltpu.VMEM((tokens, 3 * width), BF16),
        ],
        compiler_params=pltpu.CompilerParams(vmem_limit_bytes=50 * 2**20),
    )(f, g, w_qkv, w_out, vd)
    weight_grad = lax.psum_scatter(wg, ("space", "date"), scatter_dimension=0, tiled=True)
    grad_in = lax.all_to_all(gi, "date", split_axis=1, concat_axis=0, tiled=True)
    return (grad_in.transpose(1, 0, 2), weight_grad.astype(F32))


def solution(mesh):
    return jax.shard_map(
        local,
        mesh=mesh,
        in_specs=(
            P("date", ("groups", "space"), None),
            P("date", ("groups", "space"), None),
            P(),
            P(),
            P(None, ("groups", "space", "date")),
        ),
        out_specs=(P("date", ("groups", "space"), None), P(("groups", "space", "date"), None)),
        check_vma=False,
    )
```

```python
import jax
import jax.numpy as jnp
from jax import lax
from jax.experimental import pallas as pl
from jax.experimental.pallas import tpu as pltpu
from jax.sharding import PartitionSpec as P

HD = 64
epsilon = 1e-05
F32 = jnp.float32
BF16 = jnp.bfloat16
NT = (((1,), (1,)), ((), ()))
TN = (((0,), (0,)), ((), ()))
ROWS = 128


def stats(rows):
    flat = rows.astype(F32)
    centred = flat - jnp.mean(flat, axis=-1, keepdims=True)
    variance = jnp.mean(centred * centred, axis=-1, keepdims=True)
    inv_std = lax.rsqrt(variance + epsilon)
    return centred * inv_std, inv_std


def group_rows(ref, i):
    dates, width = ref.shape[1:]
    n = ROWS // dates
    return ref[pl.ds(i * n, n)].reshape(ROWS, width)


def project(i, f_ref, g_ref, wq_ref, wo_ref, nbt, qkv, da):
    normed, _ = stats(group_rows(f_ref, i))
    nb = normed.astype(BF16)
    at = pl.ds(pl.multiple_of(i * ROWS, ROWS), ROWS)
    nbt[:, at] = nb.T
    qkv[at, :] = jnp.dot(nb, wq_ref[...], preferred_element_type=F32).astype(BF16)
    da[at, :] = lax.dot_general(
        group_rows(g_ref, i), wo_ref[...], NT, preferred_element_type=F32
    ).astype(BF16)


def attend(i, dates, vd_ref, qkv, da, att, dqkv):
    width = da.shape[1]
    scale = 1.0 / HD**0.5
    at = pl.ds(pl.multiple_of(i * ROWS, ROWS), ROWS)
    row = lax.broadcasted_iota(jnp.int32, (ROWS, ROWS), 0)
    col = lax.broadcasted_iota(jnp.int32, (ROWS, ROWS), 1)
    keep = ((row // dates) == (col // dates)) & ((vd_ref[i] == 1) | (row == col))
    bias = jnp.where(keep, 0.0, -1e30).astype(F32)
    bias = jnp.concatenate([bias, bias], axis=0)
    lane = lax.broadcasted_iota(jnp.int32, (1, 2 * HD), 1)
    first = jnp.where(lane < HD, 1.0, 0.0).astype(BF16)
    second = jnp.where(lane < HD, 0.0, 1.0).astype(BF16)

    def stack(a):
        return jnp.concatenate([a * first, a * second], axis=0)

    def side(a):
        return jnp.concatenate([a[:ROWS], a[ROWS:]], axis=1)

    for c in range(0, width, 2 * HD):
        q = stack(qkv[at, c : c + 2 * HD])
        k = qkv[at, width + c : width + c + 2 * HD]
        v = qkv[at, 2 * width + c : 2 * width + c + 2 * HD]
        d = stack(da[at, c : c + 2 * HD])
        s = lax.dot_general(q, k, NT, preferred_element_type=F32) * scale + bias
        e = jnp.exp(s - jnp.max(s, axis=-1, keepdims=True))
        prob = e / jnp.sum(e, axis=-1, keepdims=True)
        prob_b = prob.astype(BF16)
        o = jnp.dot(side(prob_b), stack(v), preferred_element_type=F32).astype(BF16)
        att[c : c + 2 * HD, at] = o.T
        dp = lax.dot_general(d, v, NT, preferred_element_type=F32)
        delta = jnp.sum(prob * dp, axis=-1, keepdims=True)
        ds = (prob * (dp - delta) * scale).astype(BF16)
        dqkv[at, c : c + 2 * HD] = jnp.dot(
            side(ds), stack(k), preferred_element_type=F32
        ).astype(BF16)
        dqkv[at, width + c : width + c + 2 * HD] = lax.dot_general(
            ds, q, TN, preferred_element_type=F32
        ).astype(BF16)
        dqkv[at, 2 * width + c : 2 * width + c + 2 * HD] = lax.dot_general(
            prob_b, d, TN, preferred_element_type=F32
        ).astype(BF16)


def norm_backward(i, f_ref, g_ref, wq_ref, dqkv):
    at = pl.ds(pl.multiple_of(i * ROWS, ROWS), ROWS)
    dn = lax.dot_general(dqkv[at, :], wq_ref[...], NT, preferred_element_type=F32)
    normed, inv_std = stats(group_rows(f_ref, i))
    first = jnp.mean(dn, axis=-1, keepdims=True)
    second = jnp.mean(dn * normed, axis=-1, keepdims=True)
    return (group_rows(g_ref, i).astype(F32) + inv_std * (dn - first - normed * second)).astype(
        BF16
    )


def compute_kernel(f_ref, g_ref, wq_ref, wo_ref, vd_ref, gi_ref, wg_ref, nbt, qkv, da, att, dqkv):
    patches, dates, width = f_ref.shape
    groups = patches * dates // ROWS
    n = ROWS // dates

    @pl.loop(0, groups)
    def _(i):
        project(i, f_ref, g_ref, wq_ref, wo_ref, nbt, qkv, da)
        attend(i, dates, vd_ref, qkv, da, att, dqkv)
        gi_ref[pl.ds(i * n, n)] = norm_backward(i, f_ref, g_ref, wq_ref, dqkv).reshape(
            n, dates, width
        )

    tile = 256

    @pl.loop(0, 3 * width // tile)
    def _(j):
        at = pl.ds(pl.multiple_of(j * tile, tile), tile)
        wg_ref[:, at] = jnp.dot(nbt[...], dqkv[:, at], preferred_element_type=F32).astype(BF16)

    for j in range(0, width, tile):
        g = g_ref[:, :, j : j + tile].reshape(patches * dates, tile)
        wg_ref[:, 3 * width + j : 3 * width + j + tile] = jnp.dot(
            att[...], g, preferred_element_type=F32
        ).astype(BF16)


def local_plain(features, grad_out, w_qkv, w_out, valid_dates):
    width = features.shape[-1]
    dates, patches = valid_dates.shape
    tokens = dates * patches
    f = lax.all_to_all(features.transpose(1, 0, 2), "date", split_axis=0, concat_axis=1, tiled=True)
    g = lax.all_to_all(grad_out.transpose(1, 0, 2), "date", split_axis=0, concat_axis=1, tiled=True)
    vd = valid_dates.T.reshape(tokens // ROWS, 1, ROWS)
    vmem = pl.BlockSpec(memory_space=pltpu.VMEM)
    gi, wg = pl.pallas_call(
        compute_kernel,
        out_shape=(
            jax.ShapeDtypeStruct((patches, dates, width), BF16),
            jax.ShapeDtypeStruct((width, 4 * width), BF16),
        ),
        in_specs=[vmem] * 5,
        out_specs=(vmem, vmem),
        scratch_shapes=[
            pltpu.VMEM((width, tokens), BF16),
            pltpu.VMEM((tokens, 3 * width), BF16),
            pltpu.VMEM((tokens, width), BF16),
            pltpu.VMEM((width, tokens), BF16),
            pltpu.VMEM((tokens, 3 * width), BF16),
        ],
        compiler_params=pltpu.CompilerParams(vmem_limit_bytes=50 * 2**20),
    )(f, g, w_qkv, w_out, vd)
    weight_grad = lax.psum_scatter(wg, ("space", "date"), scatter_dimension=0, tiled=True)
    grad_in = lax.all_to_all(gi, "date", split_axis=1, concat_axis=0, tiled=True)
    return (grad_in.transpose(1, 0, 2), weight_grad.astype(F32))


TILE = 256
LAG = 2
MESH = pl.DeviceIdType.MESH


def full_kernel(
    f_in, g_in, wq_in, wo_in, vd_ref, gi_out, wg_out,
    f_ref, g_ref, wq_ref, wo_ref, nbt, qkv, da, att, dqkv, gi, part, core_in, core_sum, x_in, x_sum, z_in,
    load_sem, fs, fr, gs, gr, cs, cr, xs, xr, zs, zr,
):
    patches, dates, width = f_ref.shape
    near = f_in.shape[1]
    groups = patches * dates // ROWS
    n = ROWS // dates
    chunks = part.shape[0]
    spaces = x_sum.shape[1]
    inner = 3 * width // TILE
    date = lax.axis_index("date")
    space = lax.axis_index("space")
    core = lax.rem(date, 2)
    chip = date // 2
    peers = (date + 1 - 2 * core, lax.rem(date + 2, 4), 3 - date)

    def spaced(k):
        return lax.rem(space + k, spaces)

    barrier = pltpu.get_barrier_semaphore()
    for peer in peers:
        pl.semaphore_signal(barrier, inc=1, device_id={"date": peer}, device_id_type=MESH)
    for k in range(1, spaces):
        pl.semaphore_signal(barrier, inc=1, device_id={"space": spaced(k)}, device_id_type=MESH)

    here = pl.ds(pl.multiple_of(date * near, near), near)
    mine = pl.ds(date * patches, patches)
    loads = [
        pltpu.make_async_copy(f_in.at[mine], f_ref.at[:, here], load_sem.at[0]),
        pltpu.make_async_copy(g_in.at[mine], g_ref.at[:, here], load_sem.at[1]),
        pltpu.make_async_copy(wq_in, wq_ref, load_sem.at[2]),
        pltpu.make_async_copy(wo_in, wo_ref, load_sem.at[3]),
    ]
    for copy in loads:
        copy.start()
    pl.semaphore_wait(barrier, 2 + spaces)

    def forward(i, r, a):
        src, dst = ((f_in, f_ref), (g_in, g_ref))[a]
        return pltpu.make_async_remote_copy(
            src_ref=src.at[pl.ds(peers[r] * patches + i * n, n)],
            dst_ref=dst.at[pl.ds(i * n, n), here],
            send_sem=fs.at[i, r, a],
            recv_sem=fr.at[i, r, a],
            device_id={"date": peers[r]},
            device_id_type=MESH,
        )

    def backward(i, r):
        there = pl.ds(pl.multiple_of(peers[r] * near, near), near)
        return pltpu.make_async_remote_copy(
            src_ref=gi.at[pl.ds(i * n, n), there],
            dst_ref=gi_out.at[pl.ds(date * patches + i * n, n)],
            send_sem=gs.at[i, r],
            recv_sem=gr.at[i, r],
            device_id={"date": peers[r]},
            device_id_type=MESH,
        )

    def over_core(j):
        return pltpu.make_async_remote_copy(
            src_ref=part.at[j, :, :, 1 - core],
            dst_ref=core_in.at[j],
            send_sem=cs.at[j],
            recv_sem=cr.at[j],
            device_id={"date": peers[0]},
            device_id_type=MESH,
        )

    def over_chip(j):
        return pltpu.make_async_remote_copy(
            src_ref=core_sum.at[j, :, 1 - chip],
            dst_ref=x_in.at[j],
            send_sem=xs.at[j],
            recv_sem=xr.at[j],
            device_id={"date": peers[1]},
            device_id_type=MESH,
        )

    def over_space(j, k):
        return pltpu.make_async_remote_copy(
            src_ref=x_sum.at[j, spaced(k)],
            dst_ref=z_in.at[j, k - 1],
            send_sem=zs.at[j, k - 1],
            recv_sem=zr.at[j, k - 1],
            device_id={"space": spaced(k)},
            device_id_type=MESH,
        )

    @pl.loop(0, groups)
    def _(i):
        for r in (1, 2, 0):
            for a in range(2):
                forward(i, r, a).start()

    for copy in loads:
        copy.wait()

    @pl.loop(0, groups)
    def _(i):
        for r in range(3):
            for a in range(2):
                forward(i, r, a).wait_recv()
        project(i, f_ref, g_ref, wq_ref, wo_ref, nbt, qkv, da)
        attend(i, dates, vd_ref, qkv, da, att, dqkv)

    @pl.loop(0, chunks + LAG)
    def _(j):
        @pl.when(j < inner)
        def _():
            at = pl.ds(pl.multiple_of(j * TILE, TILE), TILE)
            w = jnp.dot(nbt[...], dqkv[:, at], preferred_element_type=F32).astype(BF16)
            part[j] = w.reshape(part.shape[1:])

        @pl.when((j >= inner) & (j < chunks))
        def _():
            at = pl.ds(pl.multiple_of((j - inner) * TILE, TILE), TILE)
            g = g_ref[:, :, at].reshape(patches * dates, TILE)
            w = jnp.dot(att[...], g, preferred_element_type=F32).astype(BF16)
            part[j] = w.reshape(part.shape[1:])

        @pl.when(j < chunks)
        def _():
            over_core(j).start()

        @pl.when(j >= LAG)
        def _():
            b = j - LAG
            over_core(b).wait_recv()
            total = part[b, :, :, core].astype(F32) + core_in[b].astype(F32)
            core_sum[b] = total.astype(BF16)
            over_chip(b).start()

    share = chunks // groups

    @pl.loop(0, groups)
    def _(i):
        gi[pl.ds(i * n, n)] = norm_backward(i, f_ref, g_ref, wq_ref, dqkv).reshape(n, dates, width)
        for r in (1, 2, 0):
            backward(i, r).start()

        @pl.loop(i * share, (i + 1) * share)
        def _(j):
            over_chip(j).wait_recv()
            total = core_sum[j, :, chip].astype(F32) + x_in[j].astype(F32)
            x_sum[j] = total.astype(BF16)
            for k in range(1, spaces):
                over_space(j, k).start()

    own = pltpu.make_async_copy(gi.at[:, here], gi_out.at[mine], load_sem.at[0])
    own.start()

    @pl.loop(0, chunks)
    def _(j):
        total = x_sum[j, space].astype(F32)
        for k in range(1, spaces):
            over_space(j, k).wait_recv()
            total += z_in[j, k - 1].astype(F32)
        wg_out[:, pl.ds(pl.multiple_of(j * TILE, TILE), TILE)] = total
        over_core(j).wait_send()
        over_chip(j).wait_send()
        for k in range(1, spaces):
            over_space(j, k).wait_send()

    own.wait()

    @pl.loop(0, groups)
    def _(i):
        for r in range(3):
            backward(i, r).wait()
            for a in range(2):
                forward(i, r, a).wait_send()


def local_full(features, grad_out, w_qkv, w_out, valid_dates):
    width = features.shape[-1]
    dates, patches = valid_dates.shape
    near, wide = features.shape[:2]
    tokens = dates * patches
    groups = tokens // ROWS
    spaces = lax.axis_size("space")
    chunks = 4 * width // TILE
    rows = width // (4 * spaces)
    vd = valid_dates.T.reshape(groups, 1, ROWS)
    vmem = pl.BlockSpec(memory_space=pltpu.VMEM)
    anywhere = pl.BlockSpec(memory_space=pl.ANY)
    dma = pltpu.SemaphoreType.DMA
    gi, wg = pl.pallas_call(
        full_kernel,
        out_shape=(
            jax.ShapeDtypeStruct((wide, near, width), BF16),
            jax.ShapeDtypeStruct((rows, 4 * width), F32),
        ),
        in_specs=[anywhere] * 4 + [vmem],
        out_specs=(anywhere, vmem),
        scratch_shapes=[
            pltpu.VMEM((patches, dates, width), BF16),
            pltpu.VMEM((patches, dates, width), BF16),
            pltpu.VMEM((width, 3 * width), BF16),
            pltpu.VMEM((width, width), BF16),
            pltpu.VMEM((width, tokens), BF16),
            pltpu.VMEM((tokens, 3 * width), BF16),
            pltpu.VMEM((tokens, width), BF16),
            pltpu.VMEM((width, tokens), BF16),
            pltpu.VMEM((tokens, 3 * width), BF16),
            pltpu.VMEM((patches, dates, width), BF16),
            pltpu.VMEM((chunks, spaces, 2, 2, rows, TILE), BF16),
            pltpu.VMEM((chunks, spaces, 2, rows, TILE), BF16),
            pltpu.VMEM((chunks, spaces, 2, rows, TILE), BF16),
            pltpu.VMEM((chunks, spaces, rows, TILE), BF16),
            pltpu.VMEM((chunks, spaces, rows, TILE), BF16),
            pltpu.VMEM((chunks, spaces - 1, rows, TILE), BF16),
            dma((4,)),
            dma((groups, 3, 2)),
            dma((groups, 3, 2)),
            dma((groups, 3)),
            dma((groups, 3)),
            dma((chunks,)),
            dma((chunks,)),
            dma((chunks,)),
            dma((chunks,)),
            dma((chunks, spaces - 1)),
            dma((chunks, spaces - 1)),
        ],
        compiler_params=pltpu.CompilerParams(
            collective_id=0, has_side_effects=True, vmem_limit_bytes=56 * 2**20
        ),
    )(features.transpose(1, 0, 2), grad_out.transpose(1, 0, 2), w_qkv, w_out, vd)
    return (gi.transpose(1, 0, 2), wg)


def local(features, grad_out, w_qkv, w_out, valid_dates):
    width = features.shape[-1]
    parts = 4 * lax.axis_size("space")
    tokens = valid_dates.size
    fits = (
        lax.axis_size("date") == 4
        and width % (16 * parts) == 0
        and features.shape[0] % 16 == 0
        and (4 * width // TILE) % (tokens // ROWS) == 0
    )
    way = local_full if fits else local_plain
    return way(features, grad_out, w_qkv, w_out, valid_dates)


def solution(mesh):
    return jax.shard_map(
        local,
        mesh=mesh,
        in_specs=(
            P("date", ("groups", "space"), None),
            P("date", ("groups", "space"), None),
            P(),
            P(),
            P(None, ("groups", "space", "date")),
        ),
        out_specs=(P("date", ("groups", "space"), None), P(("groups", "space", "date"), None)),
        check_vma=False,
    )
```

```python
import jax
import jax.numpy as jnp
from jax import lax
from jax.experimental import pallas as pl
from jax.experimental.pallas import tpu as pltpu
from jax.sharding import PartitionSpec as P

HD = 64
epsilon = 1e-05
F32 = jnp.float32
BF16 = jnp.bfloat16
NT = (((1,), (1,)), ((), ()))
ROWS = 128


def stats(rows):
    flat = rows.astype(F32)
    centred = flat - jnp.mean(flat, axis=-1, keepdims=True)
    variance = jnp.mean(centred * centred, axis=-1, keepdims=True)
    inv_std = lax.rsqrt(variance + epsilon)
    return centred * inv_std, inv_std


def group_rows(ref, i):
    dates, width = ref.shape[1:]
    n = ROWS // dates
    return ref[pl.ds(i * n, n)].reshape(ROWS, width)


def project(i, f_ref, g_ref, wq_ref, wo_ref, nbt, qkv, da):
    normed, _ = stats(group_rows(f_ref, i))
    nb = normed.astype(BF16)
    at = pl.ds(pl.multiple_of(i * ROWS, ROWS), ROWS)
    nbt[:, at] = nb.T
    qkv[at, :] = jnp.dot(nb, wq_ref[...], preferred_element_type=F32).astype(BF16)
    da[at, :] = lax.dot_general(
        group_rows(g_ref, i), wo_ref[...], NT, preferred_element_type=F32
    ).astype(BF16)


def attend(i, dates, vd_ref, qkv, da, att, dqkv):
    width = da.shape[1]
    scale = 1.0 / HD**0.5
    at = pl.ds(pl.multiple_of(i * ROWS, ROWS), ROWS)
    n = ROWS // dates
    patch = lax.broadcasted_iota(jnp.int32, vd_ref.shape, 1)
    valid = vd_ref[...]
    valid = jnp.concatenate(
        [
            jnp.sum(jnp.where(patch == i * n + p, valid, 0), axis=1, keepdims=True)
            for p in range(n)
        ],
        axis=0,
    )
    row = lax.broadcasted_iota(jnp.int32, (ROWS, ROWS), 0)
    col = lax.broadcasted_iota(jnp.int32, (ROWS, ROWS), 1)
    keep = ((row // dates) == (col // dates)) & ((valid == 1) | (row == col))
    bias = jnp.where(keep, 0.0, -1e30).astype(F32)
    bias = jnp.concatenate([bias, bias], axis=1)
    lane = lax.broadcasted_iota(jnp.int32, (1, 2 * HD), 1)
    first = jnp.where(lane < HD, 1.0, 0.0)
    second = jnp.where(lane < HD, 0.0, 1.0)
    ones = (first.astype(BF16), second.astype(BF16))
    scales = ((first * scale).astype(BF16), (second * scale).astype(BF16))

    def stack(a, by):
        return jnp.concatenate([a * by[0], a * by[1]], axis=0)

    def halves(a):
        return jnp.concatenate([a[:HD, :ROWS], a[HD:, ROWS:]], axis=0).astype(BF16)

    for c in range(0, width, 2 * HD):
        q = stack(qkv[at, c : c + 2 * HD], scales)
        k = qkv[at, width + c : width + c + 2 * HD]
        v = qkv[at, 2 * width + c : 2 * width + c + 2 * HD]
        d = stack(da[at, c : c + 2 * HD], ones)
        s = lax.dot_general(k, q, NT, preferred_element_type=F32) + bias
        e = jnp.exp(s - jnp.max(s, axis=0, keepdims=True))
        prob = e * (1.0 / jnp.sum(e, axis=0, keepdims=True))
        prob_b = prob.astype(BF16)
        att[c : c + 2 * HD, at] = halves(jnp.dot(v.T, prob_b, preferred_element_type=F32))
        dp = lax.dot_general(v, d, NT, preferred_element_type=F32)
        delta = jnp.sum(prob * dp, axis=0, keepdims=True)
        ds = (prob * (dp - delta)).astype(BF16)
        k_scaled = k * jnp.asarray(scale, BF16)
        dqkv[at, c : c + 2 * HD] = halves(
            jnp.dot(k_scaled.T, ds, preferred_element_type=F32)
        ).T
        dqkv[at, width + c : width + c + 2 * HD] = jnp.dot(
            ds, q, preferred_element_type=F32
        ).astype(BF16)
        dqkv[at, 2 * width + c : 2 * width + c + 2 * HD] = jnp.dot(
            prob_b, d, preferred_element_type=F32
        ).astype(BF16)


def norm_backward(i, f_ref, g_ref, wq_ref, dqkv):
    at = pl.ds(pl.multiple_of(i * ROWS, ROWS), ROWS)
    dn = lax.dot_general(dqkv[at, :], wq_ref[...], NT, preferred_element_type=F32)
    normed, inv_std = stats(group_rows(f_ref, i))
    first = jnp.mean(dn, axis=-1, keepdims=True)
    second = jnp.mean(dn * normed, axis=-1, keepdims=True)
    return (group_rows(g_ref, i).astype(F32) + inv_std * (dn - first - normed * second)).astype(
        BF16
    )


def compute_kernel(f_ref, g_ref, wq_ref, wo_ref, vd_ref, gi_ref, wg_ref, nbt, qkv, da, att, dqkv):
    patches, dates, width = f_ref.shape
    groups = patches * dates // ROWS
    n = ROWS // dates

    @pl.loop(0, groups)
    def _(i):
        project(i, f_ref, g_ref, wq_ref, wo_ref, nbt, qkv, da)
        attend(i, dates, vd_ref, qkv, da, att, dqkv)
        gi_ref[pl.ds(i * n, n)] = norm_backward(i, f_ref, g_ref, wq_ref, dqkv).reshape(
            n, dates, width
        )

    tile = 256

    @pl.loop(0, 3 * width // tile)
    def _(j):
        at = pl.ds(pl.multiple_of(j * tile, tile), tile)
        wg_ref[:, at] = jnp.dot(nbt[...], dqkv[:, at], preferred_element_type=F32).astype(BF16)

    for j in range(0, width, tile):
        g = g_ref[:, :, j : j + tile].reshape(patches * dates, tile)
        wg_ref[:, 3 * width + j : 3 * width + j + tile] = jnp.dot(
            att[...], g, preferred_element_type=F32
        ).astype(BF16)


def local_plain(features, grad_out, w_qkv, w_out, valid_dates):
    width = features.shape[-1]
    dates, patches = valid_dates.shape
    tokens = dates * patches
    f = lax.all_to_all(features.transpose(1, 0, 2), "date", split_axis=0, concat_axis=1, tiled=True)
    g = lax.all_to_all(grad_out.transpose(1, 0, 2), "date", split_axis=0, concat_axis=1, tiled=True)
    vmem = pl.BlockSpec(memory_space=pltpu.VMEM)
    gi, wg = pl.pallas_call(
        compute_kernel,
        out_shape=(
            jax.ShapeDtypeStruct((patches, dates, width), BF16),
            jax.ShapeDtypeStruct((width, 4 * width), BF16),
        ),
        in_specs=[vmem] * 5,
        out_specs=(vmem, vmem),
        scratch_shapes=[
            pltpu.VMEM((width, tokens), BF16),
            pltpu.VMEM((tokens, 3 * width), BF16),
            pltpu.VMEM((tokens, width), BF16),
            pltpu.VMEM((width, tokens), BF16),
            pltpu.VMEM((tokens, 3 * width), BF16),
        ],
        compiler_params=pltpu.CompilerParams(vmem_limit_bytes=50 * 2**20),
    )(f, g, w_qkv, w_out, valid_dates)
    weight_grad = lax.psum_scatter(wg, ("space", "date"), scatter_dimension=0, tiled=True)
    grad_in = lax.all_to_all(gi, "date", split_axis=1, concat_axis=0, tiled=True)
    return (grad_in.transpose(1, 0, 2), weight_grad.astype(F32))


TILE = 256
LAG = 2
MESH = pl.DeviceIdType.MESH


def full_kernel(
    f_in, g_in, wq_in, wo_in, vd_ref, gi_out, wg_out,
    f_ref, g_ref, wq_ref, wo_ref, nbt, qkv, da, att, dqkv, gi, part, core_in, core_sum, x_in, x_sum, z_in,
    load_sem, fs, fr, gs, gr, cs, cr, xs, xr, zs, zr,
):
    patches, dates, width = f_ref.shape
    near = f_in.shape[1]
    groups = patches * dates // ROWS
    n = ROWS // dates
    chunks = part.shape[0]
    spaces = x_sum.shape[1]
    inner = 3 * width // TILE
    date = lax.axis_index("date")
    space = lax.axis_index("space")
    core = lax.rem(date, 2)
    chip = date // 2
    peers = (date + 1 - 2 * core, lax.rem(date + 2, 4), 3 - date)

    def spaced(k):
        return lax.rem(space + k, spaces)

    barrier = pltpu.get_barrier_semaphore()
    for peer in peers:
        pl.semaphore_signal(barrier, inc=1, device_id={"date": peer}, device_id_type=MESH)
    for k in range(1, spaces):
        pl.semaphore_signal(barrier, inc=1, device_id={"space": spaced(k)}, device_id_type=MESH)

    here = pl.ds(pl.multiple_of(date * near, near), near)
    mine = pl.ds(date * patches, patches)
    loads = [
        pltpu.make_async_copy(f_in.at[mine], f_ref.at[:, here], load_sem.at[0]),
        pltpu.make_async_copy(g_in.at[mine], g_ref.at[:, here], load_sem.at[1]),
        pltpu.make_async_copy(wq_in, wq_ref, load_sem.at[2]),
        pltpu.make_async_copy(wo_in, wo_ref, load_sem.at[3]),
    ]
    for copy in loads:
        copy.start()
    pl.semaphore_wait(barrier, 2 + spaces)

    def forward(i, r, a):
        src, dst = ((f_in, f_ref), (g_in, g_ref))[a]
        return pltpu.make_async_remote_copy(
            src_ref=src.at[pl.ds(peers[r] * patches + i * n, n)],
            dst_ref=dst.at[pl.ds(i * n, n), here],
            send_sem=fs.at[i, r, a],
            recv_sem=fr.at[i, r, a],
            device_id={"date": peers[r]},
            device_id_type=MESH,
        )

    def backward(i, r):
        there = pl.ds(pl.multiple_of(peers[r] * near, near), near)
        return pltpu.make_async_remote_copy(
            src_ref=gi.at[pl.ds(i * n, n), there],
            dst_ref=gi_out.at[pl.ds(date * patches + i * n, n)],
            send_sem=gs.at[i, r],
            recv_sem=gr.at[i, r],
            device_id={"date": peers[r]},
            device_id_type=MESH,
        )

    def over_core(j):
        return pltpu.make_async_remote_copy(
            src_ref=part.at[j, :, :, 1 - core],
            dst_ref=core_in.at[j],
            send_sem=cs.at[j],
            recv_sem=cr.at[j],
            device_id={"date": peers[0]},
            device_id_type=MESH,
        )

    def over_chip(j):
        return pltpu.make_async_remote_copy(
            src_ref=core_sum.at[j, :, 1 - chip],
            dst_ref=x_in.at[j],
            send_sem=xs.at[j],
            recv_sem=xr.at[j],
            device_id={"date": peers[1]},
            device_id_type=MESH,
        )

    def over_space(j, k):
        return pltpu.make_async_remote_copy(
            src_ref=x_sum.at[j, spaced(k)],
            dst_ref=z_in.at[j, k - 1],
            send_sem=zs.at[j, k - 1],
            recv_sem=zr.at[j, k - 1],
            device_id={"space": spaced(k)},
            device_id_type=MESH,
        )

    @pl.loop(0, groups)
    def _(i):
        for r in (1, 2, 0):
            for a in range(2):
                forward(i, r, a).start()

    for copy in loads:
        copy.wait()

    @pl.loop(0, groups)
    def _(i):
        for r in range(3):
            for a in range(2):
                forward(i, r, a).wait_recv()
        project(i, f_ref, g_ref, wq_ref, wo_ref, nbt, qkv, da)
        attend(i, dates, vd_ref, qkv, da, att, dqkv)

    @pl.loop(0, chunks + LAG)
    def _(j):
        @pl.when(j < inner)
        def _():
            at = pl.ds(pl.multiple_of(j * TILE, TILE), TILE)
            w = jnp.dot(nbt[...], dqkv[:, at], preferred_element_type=F32).astype(BF16)
            part[j] = w.reshape(part.shape[1:])

        @pl.when((j >= inner) & (j < chunks))
        def _():
            at = pl.ds(pl.multiple_of((j - inner) * TILE, TILE), TILE)
            g = g_ref[:, :, at].reshape(patches * dates, TILE)
            w = jnp.dot(att[...], g, preferred_element_type=F32).astype(BF16)
            part[j] = w.reshape(part.shape[1:])

        @pl.when(j < chunks)
        def _():
            over_core(j).start()

        @pl.when(j >= LAG)
        def _():
            b = j - LAG
            over_core(b).wait_recv()
            total = part[b, :, :, core].astype(F32) + core_in[b].astype(F32)
            core_sum[b] = total.astype(BF16)
            over_chip(b).start()

    share = chunks // groups

    @pl.loop(0, groups)
    def _(i):
        gi[pl.ds(i * n, n)] = norm_backward(i, f_ref, g_ref, wq_ref, dqkv).reshape(n, dates, width)
        for r in (1, 2, 0):
            backward(i, r).start()

        @pl.loop(i * share, (i + 1) * share)
        def _(j):
            over_chip(j).wait_recv()
            total = core_sum[j, :, chip].astype(F32) + x_in[j].astype(F32)
            x_sum[j] = total.astype(BF16)
            for k in range(1, spaces):
                over_space(j, k).start()

    own = pltpu.make_async_copy(gi.at[:, here], gi_out.at[mine], load_sem.at[0])
    own.start()

    @pl.loop(0, chunks)
    def _(j):
        total = x_sum[j, space].astype(F32)
        for k in range(1, spaces):
            over_space(j, k).wait_recv()
            total += z_in[j, k - 1].astype(F32)
        wg_out[:, pl.ds(pl.multiple_of(j * TILE, TILE), TILE)] = total
        over_core(j).wait_send()
        over_chip(j).wait_send()
        for k in range(1, spaces):
            over_space(j, k).wait_send()

    own.wait()

    @pl.loop(0, groups)
    def _(i):
        for r in range(3):
            backward(i, r).wait()
            for a in range(2):
                forward(i, r, a).wait_send()


def local_full(features, grad_out, w_qkv, w_out, valid_dates):
    width = features.shape[-1]
    dates, patches = valid_dates.shape
    near, wide = features.shape[:2]
    tokens = dates * patches
    groups = tokens // ROWS
    spaces = lax.axis_size("space")
    chunks = 4 * width // TILE
    rows = width // (4 * spaces)
    vmem = pl.BlockSpec(memory_space=pltpu.VMEM)
    anywhere = pl.BlockSpec(memory_space=pl.ANY)
    dma = pltpu.SemaphoreType.DMA
    gi, wg = pl.pallas_call(
        full_kernel,
        out_shape=(
            jax.ShapeDtypeStruct((wide, near, width), BF16),
            jax.ShapeDtypeStruct((rows, 4 * width), F32),
        ),
        in_specs=[anywhere] * 4 + [vmem],
        out_specs=(anywhere, vmem),
        scratch_shapes=[
            pltpu.VMEM((patches, dates, width), BF16),
            pltpu.VMEM((patches, dates, width), BF16),
            pltpu.VMEM((width, 3 * width), BF16),
            pltpu.VMEM((width, width), BF16),
            pltpu.VMEM((width, tokens), BF16),
            pltpu.VMEM((tokens, 3 * width), BF16),
            pltpu.VMEM((tokens, width), BF16),
            pltpu.VMEM((width, tokens), BF16),
            pltpu.VMEM((tokens, 3 * width), BF16),
            pltpu.VMEM((patches, dates, width), BF16),
            pltpu.VMEM((chunks, spaces, 2, 2, rows, TILE), BF16),
            pltpu.VMEM((chunks, spaces, 2, rows, TILE), BF16),
            pltpu.VMEM((chunks, spaces, 2, rows, TILE), BF16),
            pltpu.VMEM((chunks, spaces, rows, TILE), BF16),
            pltpu.VMEM((chunks, spaces, rows, TILE), BF16),
            pltpu.VMEM((chunks, spaces - 1, rows, TILE), BF16),
            dma((4,)),
            dma((groups, 3, 2)),
            dma((groups, 3, 2)),
            dma((groups, 3)),
            dma((groups, 3)),
            dma((chunks,)),
            dma((chunks,)),
            dma((chunks,)),
            dma((chunks,)),
            dma((chunks, spaces - 1)),
            dma((chunks, spaces - 1)),
        ],
        compiler_params=pltpu.CompilerParams(
            collective_id=0, has_side_effects=True, vmem_limit_bytes=56 * 2**20
        ),
    )(features.transpose(1, 0, 2), grad_out.transpose(1, 0, 2), w_qkv, w_out, valid_dates)
    return (gi.transpose(1, 0, 2), wg)


def local(features, grad_out, w_qkv, w_out, valid_dates):
    width = features.shape[-1]
    parts = 4 * lax.axis_size("space")
    tokens = valid_dates.size
    fits = (
        lax.axis_size("date") == 4
        and width % (16 * parts) == 0
        and features.shape[0] % 16 == 0
        and (4 * width // TILE) % (tokens // ROWS) == 0
    )
    way = local_full if fits else local_plain
    return way(features, grad_out, w_qkv, w_out, valid_dates)


def solution(mesh):
    return jax.shard_map(
        local,
        mesh=mesh,
        in_specs=(
            P("date", ("groups", "space"), None),
            P("date", ("groups", "space"), None),
            P(),
            P(),
            P(None, ("groups", "space", "date")),
        ),
        out_specs=(P("date", ("groups", "space"), None), P(("groups", "space", "date"), None)),
        check_vma=False,
    )
```

```python
import jax
import jax.numpy as jnp
from jax import lax
from jax.experimental import pallas as pl
from jax.experimental.pallas import tpu as pltpu
from jax.sharding import PartitionSpec as P

HD = 64
epsilon = 1e-05
F32 = jnp.float32
BF16 = jnp.bfloat16
NT = (((1,), (1,)), ((), ()))
ROWS = 128


def stats(rows):
    flat = rows.astype(F32)
    centred = flat - jnp.mean(flat, axis=-1, keepdims=True)
    variance = jnp.mean(centred * centred, axis=-1, keepdims=True)
    inv_std = lax.rsqrt(variance + epsilon)
    return centred * inv_std, inv_std


def group_rows(ref, i):
    dates, width = ref.shape[1:]
    n = ROWS // dates
    return ref[pl.ds(i * n, n)].reshape(ROWS, width)


def project(i, f_ref, g_ref, wq_ref, wo_ref, nbt, qkv, da):
    normed, _ = stats(group_rows(f_ref, i))
    nb = normed.astype(BF16)
    at = pl.ds(pl.multiple_of(i * ROWS, ROWS), ROWS)
    nbt[:, at] = nb.T
    qkv[at, :] = jnp.dot(nb, wq_ref[...], preferred_element_type=F32).astype(BF16)
    da[at, :] = lax.dot_general(
        group_rows(g_ref, i), wo_ref[...], NT, preferred_element_type=F32
    ).astype(BF16)


def attend(i, dates, vd_ref, qkv, da, att, dqkv):
    width = da.shape[1]
    scale = 1.0 / HD**0.5
    at = pl.ds(pl.multiple_of(i * ROWS, ROWS), ROWS)
    n = ROWS // dates
    valid = vd_ref[...].astype(F32).T
    patch = lax.broadcasted_iota(jnp.int32, valid.shape, 1)
    valid = jnp.concatenate(
        [
            jnp.sum(jnp.where(patch == i * n + p, valid, 0.0), axis=1, keepdims=True)
            for p in range(n)
        ],
        axis=0,
    )
    row = lax.broadcasted_iota(jnp.int32, (ROWS, ROWS), 0)
    col = lax.broadcasted_iota(jnp.int32, (ROWS, ROWS), 1)
    keep = ((row // dates) == (col // dates)) & ((valid == 1.0) | (row == col))
    bias = jnp.where(keep, 0.0, -1e30).astype(F32)
    bias = jnp.concatenate([bias, bias], axis=1)
    lane = lax.broadcasted_iota(jnp.int32, (1, 2 * HD), 1)
    first = jnp.where(lane < HD, 1.0, 0.0)
    second = jnp.where(lane < HD, 0.0, 1.0)
    ones = (first.astype(BF16), second.astype(BF16))
    scales = ((first * scale).astype(BF16), (second * scale).astype(BF16))

    def stack(a, by):
        return jnp.concatenate([a * by[0], a * by[1]], axis=0)

    def halves(a):
        return jnp.concatenate([a[:HD, :ROWS], a[HD:, ROWS:]], axis=0).astype(BF16)

    for c in range(0, width, 2 * HD):
        q = stack(qkv[at, c : c + 2 * HD], scales)
        k = qkv[at, width + c : width + c + 2 * HD]
        v = qkv[at, 2 * width + c : 2 * width + c + 2 * HD]
        d = stack(da[at, c : c + 2 * HD], ones)
        s = lax.dot_general(k, q, NT, preferred_element_type=F32) + bias
        e = jnp.exp(s - jnp.max(s, axis=0, keepdims=True))
        prob = e * (1.0 / jnp.sum(e, axis=0, keepdims=True))
        prob_b = prob.astype(BF16)
        att[c : c + 2 * HD, at] = halves(jnp.dot(v.T, prob_b, preferred_element_type=F32))
        dp = lax.dot_general(v, d, NT, preferred_element_type=F32)
        delta = jnp.sum(prob * dp, axis=0, keepdims=True)
        ds = (prob * (dp - delta)).astype(BF16)
        k_scaled = k * jnp.asarray(scale, BF16)
        dqkv[at, c : c + 2 * HD] = halves(
            jnp.dot(k_scaled.T, ds, preferred_element_type=F32)
        ).T
        dqkv[at, width + c : width + c + 2 * HD] = jnp.dot(
            ds, q, preferred_element_type=F32
        ).astype(BF16)
        dqkv[at, 2 * width + c : 2 * width + c + 2 * HD] = jnp.dot(
            prob_b, d, preferred_element_type=F32
        ).astype(BF16)


def norm_backward(i, f_ref, g_ref, wq_ref, dqkv):
    at = pl.ds(pl.multiple_of(i * ROWS, ROWS), ROWS)
    dn = lax.dot_general(dqkv[at, :], wq_ref[...], NT, preferred_element_type=F32)
    normed, inv_std = stats(group_rows(f_ref, i))
    first = jnp.mean(dn, axis=-1, keepdims=True)
    second = jnp.mean(dn * normed, axis=-1, keepdims=True)
    return (group_rows(g_ref, i).astype(F32) + inv_std * (dn - first - normed * second)).astype(
        BF16
    )


def compute_kernel(f_ref, g_ref, wq_ref, wo_ref, vd_ref, gi_ref, wg_ref, nbt, qkv, da, att, dqkv):
    patches, dates, width = f_ref.shape
    groups = patches * dates // ROWS
    n = ROWS // dates

    @pl.loop(0, groups)
    def _(i):
        project(i, f_ref, g_ref, wq_ref, wo_ref, nbt, qkv, da)
        attend(i, dates, vd_ref, qkv, da, att, dqkv)
        gi_ref[pl.ds(i * n, n)] = norm_backward(i, f_ref, g_ref, wq_ref, dqkv).reshape(
            n, dates, width
        )

    tile = 256

    @pl.loop(0, 3 * width // tile)
    def _(j):
        at = pl.ds(pl.multiple_of(j * tile, tile), tile)
        wg_ref[:, at] = jnp.dot(nbt[...], dqkv[:, at], preferred_element_type=F32).astype(BF16)

    for j in range(0, width, tile):
        g = g_ref[:, :, j : j + tile].reshape(patches * dates, tile)
        wg_ref[:, 3 * width + j : 3 * width + j + tile] = jnp.dot(
            att[...], g, preferred_element_type=F32
        ).astype(BF16)


def local_plain(features, grad_out, w_qkv, w_out, valid_dates):
    width = features.shape[-1]
    dates, patches = valid_dates.shape
    tokens = dates * patches
    f = lax.all_to_all(features.transpose(1, 0, 2), "date", split_axis=0, concat_axis=1, tiled=True)
    g = lax.all_to_all(grad_out.transpose(1, 0, 2), "date", split_axis=0, concat_axis=1, tiled=True)
    vmem = pl.BlockSpec(memory_space=pltpu.VMEM)
    gi, wg = pl.pallas_call(
        compute_kernel,
        out_shape=(
            jax.ShapeDtypeStruct((patches, dates, width), BF16),
            jax.ShapeDtypeStruct((width, 4 * width), BF16),
        ),
        in_specs=[vmem] * 5,
        out_specs=(vmem, vmem),
        scratch_shapes=[
            pltpu.VMEM((width, tokens), BF16),
            pltpu.VMEM((tokens, 3 * width), BF16),
            pltpu.VMEM((tokens, width), BF16),
            pltpu.VMEM((width, tokens), BF16),
            pltpu.VMEM((tokens, 3 * width), BF16),
        ],
        compiler_params=pltpu.CompilerParams(vmem_limit_bytes=50 * 2**20),
    )(f, g, w_qkv, w_out, valid_dates.T)
    weight_grad = lax.psum_scatter(wg, ("space", "date"), scatter_dimension=0, tiled=True)
    grad_in = lax.all_to_all(gi, "date", split_axis=1, concat_axis=0, tiled=True)
    return (grad_in.transpose(1, 0, 2), weight_grad.astype(F32))


TILE = 256
LAG = 2
EARLY = 2
MESH = pl.DeviceIdType.MESH


def full_kernel(
    f_in, g_in, wq_in, wo_in, vd_ref, gi_out, wg_out,
    f_ref, g_ref, wq_ref, wo_ref, nbt, qkv, da, att, dqkv, gi, part, core_in, core_sum, x_in, x_sum, z_in, early_in, early_sum, last_in,
    load_sem, fs, fr, gs, gr, cs, cr, xs, xr, zs, zr,
):
    patches, dates, width = f_ref.shape
    near = f_in.shape[1]
    groups = patches * dates // ROWS
    n = ROWS // dates
    chunks = part.shape[0]
    spaces = x_sum.shape[1]
    inner = 3 * width // TILE
    date = lax.axis_index("date")
    space = lax.axis_index("space")
    core = lax.rem(date, 2)
    chip = date // 2
    peers = (date + 1 - 2 * core, lax.rem(date + 2, 4), 3 - date)

    def spaced(k):
        return lax.rem(space + k, spaces)

    barrier = pltpu.get_barrier_semaphore()
    for peer in peers:
        pl.semaphore_signal(barrier, inc=1, device_id={"date": peer}, device_id_type=MESH)
    for k in range(1, spaces):
        pl.semaphore_signal(barrier, inc=1, device_id={"space": spaced(k)}, device_id_type=MESH)

    here = pl.ds(pl.multiple_of(date * near, near), near)
    mine = pl.ds(date * patches, patches)
    loads = [
        pltpu.make_async_copy(f_in.at[mine], f_ref.at[:, here], load_sem.at[0]),
        pltpu.make_async_copy(g_in.at[mine], g_ref.at[:, here], load_sem.at[1]),
        pltpu.make_async_copy(wq_in, wq_ref, load_sem.at[2]),
        pltpu.make_async_copy(wo_in, wo_ref, load_sem.at[3]),
    ]
    for copy in loads:
        copy.start()
    pl.semaphore_wait(barrier, 2 + spaces)

    def forward(i, r, a):
        src, dst = ((f_in, f_ref), (g_in, g_ref))[a]
        return pltpu.make_async_remote_copy(
            src_ref=src.at[pl.ds(peers[r] * patches + i * n, n)],
            dst_ref=dst.at[pl.ds(i * n, n), here],
            send_sem=fs.at[i, r, a],
            recv_sem=fr.at[i, r, a],
            device_id={"date": peers[r]},
            device_id_type=MESH,
        )

    def backward(i, r):
        there = pl.ds(pl.multiple_of(peers[r] * near, near), near)
        return pltpu.make_async_remote_copy(
            src_ref=gi.at[pl.ds(i * n, n), there],
            dst_ref=gi_out.at[pl.ds(date * patches + i * n, n)],
            send_sem=gs.at[i, r],
            recv_sem=gr.at[i, r],
            device_id={"date": peers[r]},
            device_id_type=MESH,
        )

    def over_core(j):
        return pltpu.make_async_remote_copy(
            src_ref=part.at[j, :, :, 1 - core],
            dst_ref=core_in.at[j],
            send_sem=cs.at[j],
            recv_sem=cr.at[j],
            device_id={"date": peers[0]},
            device_id_type=MESH,
        )

    def over_chip(j):
        return pltpu.make_async_remote_copy(
            src_ref=core_sum.at[j, :, 1 - chip],
            dst_ref=x_in.at[j],
            send_sem=xs.at[j],
            recv_sem=xr.at[j],
            device_id={"date": peers[1]},
            device_id_type=MESH,
        )

    def over_space(j, k):
        return pltpu.make_async_remote_copy(
            src_ref=x_sum.at[j, spaced(k)],
            dst_ref=z_in.at[j, k - 1],
            send_sem=zs.at[j, k - 1],
            recv_sem=zr.at[j, k - 1],
            device_id={"space": spaced(k)},
            device_id_type=MESH,
        )

    def early_space(j, k):
        return pltpu.make_async_remote_copy(
            src_ref=core_sum.at[j, spaced(k)],
            dst_ref=early_in.at[j, k - 1],
            send_sem=zs.at[j, k - 1],
            recv_sem=zr.at[j, k - 1],
            device_id={"space": spaced(k)},
            device_id_type=MESH,
        )

    def late_chip(j):
        return pltpu.make_async_remote_copy(
            src_ref=early_sum.at[j, 1 - chip],
            dst_ref=last_in.at[j],
            send_sem=xs.at[j],
            recv_sem=xr.at[j],
            device_id={"date": peers[1]},
            device_id_type=MESH,
        )

    @pl.loop(0, groups)
    def _(i):
        for r in (1, 2, 0):
            for a in range(2):
                forward(i, r, a).start()

    for copy in loads:
        copy.wait()

    @pl.loop(0, groups)
    def _(i):
        for r in range(3):
            for a in range(2):
                forward(i, r, a).wait_recv()
        project(i, f_ref, g_ref, wq_ref, wo_ref, nbt, qkv, da)
        attend(i, dates, vd_ref, qkv, da, att, dqkv)

    @pl.loop(0, chunks + LAG)
    def _(j):
        @pl.when(j < inner)
        def _():
            at = pl.ds(pl.multiple_of(j * TILE, TILE), TILE)
            w = jnp.dot(nbt[...], dqkv[:, at], preferred_element_type=F32).astype(BF16)
            part[j] = w.reshape(part.shape[1:])

        @pl.when((j >= inner) & (j < chunks))
        def _():
            at = pl.ds(pl.multiple_of((j - inner) * TILE, TILE), TILE)
            g = g_ref[:, :, at].reshape(patches * dates, TILE)
            w = jnp.dot(att[...], g, preferred_element_type=F32).astype(BF16)
            part[j] = w.reshape(part.shape[1:])

        @pl.when(j < chunks)
        def _():
            over_core(j).start()

        @pl.when(j >= LAG)
        def _():
            b = j - LAG
            over_core(b).wait_recv()
            total = part[b, :, :, core].astype(F32) + core_in[b].astype(F32)
            core_sum[b] = total.astype(BF16)

            @pl.when(b < EARLY)
            def _():
                for k in range(1, spaces):
                    early_space(b, k).start()

            @pl.when(b >= EARLY)
            def _():
                over_chip(b).start()

    share = chunks // groups

    @pl.loop(0, groups)
    def _(i):
        gi[pl.ds(i * n, n)] = norm_backward(i, f_ref, g_ref, wq_ref, dqkv).reshape(n, dates, width)
        for r in (1, 2, 0):
            backward(i, r).start()

        @pl.when(i == 1)
        def _():
            @pl.loop(0, EARLY)
            def _(j):
                total = core_sum[j, space].astype(F32)
                for k in range(1, spaces):
                    early_space(j, k).wait_recv()
                    total += early_in[j, k - 1].astype(F32)
                early_sum[j] = total.astype(BF16)
                late_chip(j).start()

        @pl.loop(i * share, (i + 1) * share)
        def _(j):
            @pl.when(j >= EARLY)
            def _():
                over_chip(j).wait_recv()
                total = core_sum[j, :, chip].astype(F32) + x_in[j].astype(F32)
                x_sum[j] = total.astype(BF16)
                for k in range(1, spaces):
                    over_space(j, k).start()

    own = pltpu.make_async_copy(gi.at[:, here], gi_out.at[mine], load_sem.at[0])
    own.start()

    @pl.loop(EARLY, chunks)
    def _(j):
        total = x_sum[j, space].astype(F32)
        for k in range(1, spaces):
            over_space(j, k).wait_recv()
            total += z_in[j, k - 1].astype(F32)
        wg_out[:, pl.ds(pl.multiple_of(j * TILE, TILE), TILE)] = total
        over_core(j).wait_send()
        over_chip(j).wait_send()
        for k in range(1, spaces):
            over_space(j, k).wait_send()

    @pl.loop(0, EARLY)
    def _(j):
        late_chip(j).wait_recv()
        total = early_sum[j, chip].astype(F32) + last_in[j].astype(F32)
        wg_out[:, pl.ds(pl.multiple_of(j * TILE, TILE), TILE)] = total
        over_core(j).wait_send()
        late_chip(j).wait_send()
        for k in range(1, spaces):
            early_space(j, k).wait_send()

    own.wait()

    @pl.loop(0, groups)
    def _(i):
        for r in range(3):
            backward(i, r).wait()
            for a in range(2):
                forward(i, r, a).wait_send()


def local_full(features, grad_out, w_qkv, w_out, valid_dates):
    width = features.shape[-1]
    dates, patches = valid_dates.shape
    near, wide = features.shape[:2]
    tokens = dates * patches
    groups = tokens // ROWS
    spaces = lax.axis_size("space")
    chunks = 4 * width // TILE
    rows = width // (4 * spaces)
    vmem = pl.BlockSpec(memory_space=pltpu.VMEM)
    anywhere = pl.BlockSpec(memory_space=pl.ANY)
    dma = pltpu.SemaphoreType.DMA
    gi, wg = pl.pallas_call(
        full_kernel,
        out_shape=(
            jax.ShapeDtypeStruct((wide, near, width), BF16),
            jax.ShapeDtypeStruct((rows, 4 * width), F32),
        ),
        in_specs=[anywhere] * 4 + [vmem],
        out_specs=(anywhere, vmem),
        scratch_shapes=[
            pltpu.VMEM((patches, dates, width), BF16),
            pltpu.VMEM((patches, dates, width), BF16),
            pltpu.VMEM((width, 3 * width), BF16),
            pltpu.VMEM((width, width), BF16),
            pltpu.VMEM((width, tokens), BF16),
            pltpu.VMEM((tokens, 3 * width), BF16),
            pltpu.VMEM((tokens, width), BF16),
            pltpu.VMEM((width, tokens), BF16),
            pltpu.VMEM((tokens, 3 * width), BF16),
            pltpu.VMEM((patches, dates, width), BF16),
            pltpu.VMEM((chunks, spaces, 2, 2, rows, TILE), BF16),
            pltpu.VMEM((chunks, spaces, 2, rows, TILE), BF16),
            pltpu.VMEM((chunks, spaces, 2, rows, TILE), BF16),
            pltpu.VMEM((chunks, spaces, rows, TILE), BF16),
            pltpu.VMEM((chunks, spaces, rows, TILE), BF16),
            pltpu.VMEM((chunks, spaces - 1, rows, TILE), BF16),
            pltpu.VMEM((EARLY, spaces - 1, 2, rows, TILE), BF16),
            pltpu.VMEM((EARLY, 2, rows, TILE), BF16),
            pltpu.VMEM((EARLY, rows, TILE), BF16),
            dma((4,)),
            dma((groups, 3, 2)),
            dma((groups, 3, 2)),
            dma((groups, 3)),
            dma((groups, 3)),
            dma((chunks,)),
            dma((chunks,)),
            dma((chunks,)),
            dma((chunks,)),
            dma((chunks, spaces - 1)),
            dma((chunks, spaces - 1)),
        ],
        compiler_params=pltpu.CompilerParams(
            collective_id=0, has_side_effects=True, vmem_limit_bytes=56 * 2**20
        ),
    )(features.transpose(1, 0, 2), grad_out.transpose(1, 0, 2), w_qkv, w_out, valid_dates.T)
    return (gi.transpose(1, 0, 2), wg)


def local(features, grad_out, w_qkv, w_out, valid_dates):
    width = features.shape[-1]
    parts = 4 * lax.axis_size("space")
    tokens = valid_dates.size
    fits = (
        lax.axis_size("date") == 4
        and width % (16 * parts) == 0
        and features.shape[0] % 16 == 0
        and (4 * width // TILE) % (tokens // ROWS) == 0
        and 4 * width // TILE >= EARLY * (tokens // ROWS)
        and tokens >= 2 * ROWS
    )
    way = local_full if fits else local_plain
    return way(features, grad_out, w_qkv, w_out, valid_dates)


def solution(mesh):
    return jax.shard_map(
        local,
        mesh=mesh,
        in_specs=(
            P("date", ("groups", "space"), None),
            P("date", ("groups", "space"), None),
            P(),
            P(),
            P(None, ("groups", "space", "date")),
        ),
        out_specs=(P("date", ("groups", "space"), None), P(("groups", "space", "date"), None)),
        check_vma=False,
    )
```

```python
import jax
import jax.numpy as jnp
from jax import lax
from jax.experimental import pallas as pl
from jax.experimental.pallas import tpu as pltpu
from jax.sharding import PartitionSpec as P

HD = 64
epsilon = 1e-05
F32 = jnp.float32
BF16 = jnp.bfloat16
NT = (((1,), (1,)), ((), ()))
ROWS = 128


def stats(rows):
    flat = rows.astype(F32)
    centred = flat - jnp.mean(flat, axis=-1, keepdims=True)
    variance = jnp.mean(centred * centred, axis=-1, keepdims=True)
    inv_std = lax.rsqrt(variance + epsilon)
    return centred * inv_std, inv_std


def group_rows(ref, i):
    dates, width = ref.shape[1:]
    n = ROWS // dates
    return ref[pl.ds(i * n, n)].reshape(ROWS, width)


def project(i, f_ref, g_ref, wq_ref, wo_ref, nbt, qkv, da):
    normed, _ = stats(group_rows(f_ref, i))
    nb = normed.astype(BF16)
    at = pl.ds(pl.multiple_of(i * ROWS, ROWS), ROWS)
    nbt[:, at] = nb.T
    qkv[at, :] = jnp.dot(nb, wq_ref[...], preferred_element_type=F32).astype(BF16)
    da[at, :] = lax.dot_general(
        group_rows(g_ref, i), wo_ref[...], NT, preferred_element_type=F32
    ).astype(BF16)


def attend(i, dates, vd_ref, qkv, da, att, dqkv):
    width = da.shape[1]
    scale = 1.0 / HD**0.5
    at = pl.ds(pl.multiple_of(i * ROWS, ROWS), ROWS)
    n = ROWS // dates
    valid = vd_ref[...].astype(F32).T
    patch = lax.broadcasted_iota(jnp.int32, valid.shape, 1)
    valid = jnp.concatenate(
        [
            jnp.sum(jnp.where(patch == i * n + p, valid, 0.0), axis=1, keepdims=True)
            for p in range(n)
        ],
        axis=0,
    )
    row = lax.broadcasted_iota(jnp.int32, (ROWS, ROWS), 0)
    col = lax.broadcasted_iota(jnp.int32, (ROWS, ROWS), 1)
    keep = ((row // dates) == (col // dates)) & ((valid == 1.0) | (row == col))
    bias = jnp.where(keep, 0.0, -1e30).astype(F32)
    bias = jnp.concatenate([bias, bias], axis=1)
    lane = lax.broadcasted_iota(jnp.int32, (1, 2 * HD), 1)
    first = jnp.where(lane < HD, 1.0, 0.0)
    second = jnp.where(lane < HD, 0.0, 1.0)
    ones = (first.astype(BF16), second.astype(BF16))
    scales = ((first * scale).astype(BF16), (second * scale).astype(BF16))

    def stack(a, by):
        return jnp.concatenate([a * by[0], a * by[1]], axis=0)

    def halves(a):
        return jnp.concatenate([a[:HD, :ROWS], a[HD:, ROWS:]], axis=0).astype(BF16)

    for c in range(0, width, 2 * HD):
        q = stack(qkv[at, c : c + 2 * HD], scales)
        k = qkv[at, width + c : width + c + 2 * HD]
        v = qkv[at, 2 * width + c : 2 * width + c + 2 * HD]
        d = stack(da[at, c : c + 2 * HD], ones)
        s = lax.dot_general(k, q, NT, preferred_element_type=F32) + bias
        e = jnp.exp(s - jnp.max(s, axis=0, keepdims=True))
        prob = e * (1.0 / jnp.sum(e, axis=0, keepdims=True))
        prob_b = prob.astype(BF16)
        att[c : c + 2 * HD, at] = halves(jnp.dot(v.T, prob_b, preferred_element_type=F32))
        dp = lax.dot_general(v, d, NT, preferred_element_type=F32)
        delta = jnp.sum(prob * dp, axis=0, keepdims=True)
        ds = (prob * (dp - delta)).astype(BF16)
        k_scaled = k * jnp.asarray(scale, BF16)
        dqkv[at, c : c + 2 * HD] = halves(
            jnp.dot(k_scaled.T, ds, preferred_element_type=F32)
        ).T
        dqkv[at, width + c : width + c + 2 * HD] = jnp.dot(
            ds, q, preferred_element_type=F32
        ).astype(BF16)
        dqkv[at, 2 * width + c : 2 * width + c + 2 * HD] = jnp.dot(
            prob_b, d, preferred_element_type=F32
        ).astype(BF16)


def norm_backward(i, f_ref, g_ref, wq_ref, dqkv):
    at = pl.ds(pl.multiple_of(i * ROWS, ROWS), ROWS)
    dn = lax.dot_general(dqkv[at, :], wq_ref[...], NT, preferred_element_type=F32)
    normed, inv_std = stats(group_rows(f_ref, i))
    first = jnp.mean(dn, axis=-1, keepdims=True)
    second = jnp.mean(dn * normed, axis=-1, keepdims=True)
    return (group_rows(g_ref, i).astype(F32) + inv_std * (dn - first - normed * second)).astype(
        BF16
    )


def compute_kernel(f_ref, g_ref, wq_ref, wo_ref, vd_ref, gi_ref, wg_ref, nbt, qkv, da, att, dqkv):
    patches, dates, width = f_ref.shape
    groups = patches * dates // ROWS
    n = ROWS // dates

    @pl.loop(0, groups)
    def _(i):
        project(i, f_ref, g_ref, wq_ref, wo_ref, nbt, qkv, da)
        attend(i, dates, vd_ref, qkv, da, att, dqkv)
        gi_ref[pl.ds(i * n, n)] = norm_backward(i, f_ref, g_ref, wq_ref, dqkv).reshape(
            n, dates, width
        )

    tile = 256

    @pl.loop(0, 3 * width // tile)
    def _(j):
        at = pl.ds(pl.multiple_of(j * tile, tile), tile)
        wg_ref[:, at] = jnp.dot(nbt[...], dqkv[:, at], preferred_element_type=F32).astype(BF16)

    for j in range(0, width, tile):
        g = g_ref[:, :, j : j + tile].reshape(patches * dates, tile)
        wg_ref[:, 3 * width + j : 3 * width + j + tile] = jnp.dot(
            att[...], g, preferred_element_type=F32
        ).astype(BF16)


def local_plain(features, grad_out, w_qkv, w_out, valid_dates):
    width = features.shape[-1]
    dates, patches = valid_dates.shape
    tokens = dates * patches
    f = lax.all_to_all(features.transpose(1, 0, 2), "date", split_axis=0, concat_axis=1, tiled=True)
    g = lax.all_to_all(grad_out.transpose(1, 0, 2), "date", split_axis=0, concat_axis=1, tiled=True)
    vmem = pl.BlockSpec(memory_space=pltpu.VMEM)
    gi, wg = pl.pallas_call(
        compute_kernel,
        out_shape=(
            jax.ShapeDtypeStruct((patches, dates, width), BF16),
            jax.ShapeDtypeStruct((width, 4 * width), BF16),
        ),
        in_specs=[vmem] * 5,
        out_specs=(vmem, vmem),
        scratch_shapes=[
            pltpu.VMEM((width, tokens), BF16),
            pltpu.VMEM((tokens, 3 * width), BF16),
            pltpu.VMEM((tokens, width), BF16),
            pltpu.VMEM((width, tokens), BF16),
            pltpu.VMEM((tokens, 3 * width), BF16),
        ],
        compiler_params=pltpu.CompilerParams(vmem_limit_bytes=50 * 2**20),
    )(f, g, w_qkv, w_out, valid_dates.T)
    weight_grad = lax.psum_scatter(wg, ("space", "date"), scatter_dimension=0, tiled=True)
    grad_in = lax.all_to_all(gi, "date", split_axis=1, concat_axis=0, tiled=True)
    return (grad_in.transpose(1, 0, 2), weight_grad.astype(F32))


TILE = 256
LAG = 2
EARLY = 1
MESH = pl.DeviceIdType.MESH


def full_kernel(
    f_in, g_in, wq_in, wo_in, vd_ref, gi_out, wg_out,
    f_ref, g_ref, wq_ref, wo_ref, nbt, qkv, da, att, dqkv, gi, part, core_in, core_sum, x_in, x_sum, z_in, early_in, early_sum, last_in,
    load_sem, fs, fr, gs, gr, cs, cr, xs, xr, zs, zr,
):
    patches, dates, width = f_ref.shape
    near = f_in.shape[1]
    groups = patches * dates // ROWS
    n = ROWS // dates
    chunks = part.shape[0]
    spaces = x_sum.shape[1]
    inner = 3 * width // TILE
    date = lax.axis_index("date")
    space = lax.axis_index("space")
    core = lax.rem(date, 2)
    chip = date // 2
    peers = (date + 1 - 2 * core, lax.rem(date + 2, 4), 3 - date)

    def spaced(k):
        return lax.rem(space + k, spaces)

    barrier = pltpu.get_barrier_semaphore()
    for peer in peers:
        pl.semaphore_signal(barrier, inc=1, device_id={"date": peer}, device_id_type=MESH)
    for k in range(1, spaces):
        pl.semaphore_signal(barrier, inc=1, device_id={"space": spaced(k)}, device_id_type=MESH)

    here = pl.ds(pl.multiple_of(date * near, near), near)
    mine = pl.ds(date * patches, patches)
    loads = [
        pltpu.make_async_copy(f_in.at[mine], f_ref.at[:, here], load_sem.at[0]),
        pltpu.make_async_copy(g_in.at[mine], g_ref.at[:, here], load_sem.at[1]),
        pltpu.make_async_copy(wq_in, wq_ref, load_sem.at[2]),
        pltpu.make_async_copy(wo_in, wo_ref, load_sem.at[3]),
    ]
    for copy in loads:
        copy.start()
    pl.semaphore_wait(barrier, 2 + spaces)

    def forward(i, r, a):
        src, dst = ((f_in, f_ref), (g_in, g_ref))[a]
        return pltpu.make_async_remote_copy(
            src_ref=src.at[pl.ds(peers[r] * patches + i * n, n)],
            dst_ref=dst.at[pl.ds(i * n, n), here],
            send_sem=fs.at[i, r, a],
            recv_sem=fr.at[i, r, a],
            device_id={"date": peers[r]},
            device_id_type=MESH,
        )

    def backward(i, r):
        there = pl.ds(pl.multiple_of(peers[r] * near, near), near)
        return pltpu.make_async_remote_copy(
            src_ref=gi.at[pl.ds(i * n, n), there],
            dst_ref=gi_out.at[pl.ds(date * patches + i * n, n)],
            send_sem=gs.at[i, r],
            recv_sem=gr.at[i, r],
            device_id={"date": peers[r]},
            device_id_type=MESH,
        )

    def over_core(j):
        return pltpu.make_async_remote_copy(
            src_ref=part.at[j, :, :, 1 - core],
            dst_ref=core_in.at[j],
            send_sem=cs.at[j],
            recv_sem=cr.at[j],
            device_id={"date": peers[0]},
            device_id_type=MESH,
        )

    def over_chip(j):
        return pltpu.make_async_remote_copy(
            src_ref=core_sum.at[j, :, 1 - chip],
            dst_ref=x_in.at[j],
            send_sem=xs.at[j],
            recv_sem=xr.at[j],
            device_id={"date": peers[1]},
            device_id_type=MESH,
        )

    def over_space(j, k):
        return pltpu.make_async_remote_copy(
            src_ref=x_sum.at[j, spaced(k)],
            dst_ref=z_in.at[j, k - 1],
            send_sem=zs.at[j, k - 1],
            recv_sem=zr.at[j, k - 1],
            device_id={"space": spaced(k)},
            device_id_type=MESH,
        )

    def early_space(j, k):
        return pltpu.make_async_remote_copy(
            src_ref=core_sum.at[j, spaced(k)],
            dst_ref=early_in.at[j, k - 1],
            send_sem=zs.at[j, k - 1],
            recv_sem=zr.at[j, k - 1],
            device_id={"space": spaced(k)},
            device_id_type=MESH,
        )

    def late_chip(j):
        return pltpu.make_async_remote_copy(
            src_ref=early_sum.at[j, 1 - chip],
            dst_ref=last_in.at[j],
            send_sem=xs.at[j],
            recv_sem=xr.at[j],
            device_id={"date": peers[1]},
            device_id_type=MESH,
        )

    @pl.loop(0, groups)
    def _(i):
        for r in (1, 2, 0):
            for a in range(2):
                forward(i, r, a).start()

    for copy in loads:
        copy.wait()

    def give_back(i):
        gi[pl.ds(i * n, n)] = norm_backward(i, f_ref, g_ref, wq_ref, dqkv).reshape(n, dates, width)
        for r in (1, 2, 0):
            backward(i, r).start()

    @pl.loop(0, groups)
    def _(i):
        @pl.when(i > 0)
        def _():
            give_back(i - 1)

        for r in range(3):
            for a in range(2):
                forward(i, r, a).wait_recv()
        project(i, f_ref, g_ref, wq_ref, wo_ref, nbt, qkv, da)
        attend(i, dates, vd_ref, qkv, da, att, dqkv)

    @pl.loop(0, chunks + LAG)
    def _(j):
        @pl.when(j < inner)
        def _():
            at = pl.ds(pl.multiple_of(j * TILE, TILE), TILE)
            w = jnp.dot(nbt[...], dqkv[:, at], preferred_element_type=F32).astype(BF16)
            part[j] = w.reshape(part.shape[1:])

        @pl.when((j >= inner) & (j < chunks))
        def _():
            at = pl.ds(pl.multiple_of((j - inner) * TILE, TILE), TILE)
            g = g_ref[:, :, at].reshape(patches * dates, TILE)
            w = jnp.dot(att[...], g, preferred_element_type=F32).astype(BF16)
            part[j] = w.reshape(part.shape[1:])

        @pl.when(j < chunks)
        def _():
            over_core(j).start()

        @pl.when(j >= LAG)
        def _():
            b = j - LAG
            over_core(b).wait_recv()
            total = part[b, :, :, core].astype(F32) + core_in[b].astype(F32)
            core_sum[b] = total.astype(BF16)

            @pl.when(b < EARLY)
            def _():
                for k in range(1, spaces):
                    early_space(b, k).start()

            @pl.when(b >= EARLY)
            def _():
                over_chip(b).start()

    share = chunks // groups

    @pl.loop(0, groups)
    def _(i):
        @pl.when(i == 0)
        def _():
            give_back(groups - 1)

        @pl.when(i == 1)
        def _():
            @pl.loop(0, EARLY)
            def _(j):
                total = core_sum[j, space].astype(F32)
                for k in range(1, spaces):
                    early_space(j, k).wait_recv()
                    total += early_in[j, k - 1].astype(F32)
                early_sum[j] = total.astype(BF16)
                late_chip(j).start()

        @pl.loop(i * share, (i + 1) * share)
        def _(j):
            @pl.when(j >= EARLY)
            def _():
                over_chip(j).wait_recv()
                total = core_sum[j, :, chip].astype(F32) + x_in[j].astype(F32)
                x_sum[j] = total.astype(BF16)
                for k in range(1, spaces):
                    over_space(j, k).start()

    own = pltpu.make_async_copy(gi.at[:, here], gi_out.at[mine], load_sem.at[0])
    own.start()

    @pl.loop(EARLY, chunks)
    def _(j):
        total = x_sum[j, space].astype(F32)
        for k in range(1, spaces):
            over_space(j, k).wait_recv()
            total += z_in[j, k - 1].astype(F32)
        wg_out[:, pl.ds(pl.multiple_of(j * TILE, TILE), TILE)] = total
        over_core(j).wait_send()
        over_chip(j).wait_send()
        for k in range(1, spaces):
            over_space(j, k).wait_send()

    @pl.loop(0, EARLY)
    def _(j):
        late_chip(j).wait_recv()
        total = early_sum[j, chip].astype(F32) + last_in[j].astype(F32)
        wg_out[:, pl.ds(pl.multiple_of(j * TILE, TILE), TILE)] = total
        over_core(j).wait_send()
        late_chip(j).wait_send()
        for k in range(1, spaces):
            early_space(j, k).wait_send()

    own.wait()

    @pl.loop(0, groups)
    def _(i):
        for r in range(3):
            backward(i, r).wait()
            for a in range(2):
                forward(i, r, a).wait_send()


def local_full(features, grad_out, w_qkv, w_out, valid_dates):
    width = features.shape[-1]
    dates, patches = valid_dates.shape
    near, wide = features.shape[:2]
    tokens = dates * patches
    groups = tokens // ROWS
    spaces = lax.axis_size("space")
    chunks = 4 * width // TILE
    rows = width // (4 * spaces)
    vmem = pl.BlockSpec(memory_space=pltpu.VMEM)
    anywhere = pl.BlockSpec(memory_space=pl.ANY)
    dma = pltpu.SemaphoreType.DMA
    gi, wg = pl.pallas_call(
        full_kernel,
        out_shape=(
            jax.ShapeDtypeStruct((wide, near, width), BF16),
            jax.ShapeDtypeStruct((rows, 4 * width), F32),
        ),
        in_specs=[anywhere] * 4 + [vmem],
        out_specs=(anywhere, vmem),
        scratch_shapes=[
            pltpu.VMEM((patches, dates, width), BF16),
            pltpu.VMEM((patches, dates, width), BF16),
            pltpu.VMEM((width, 3 * width), BF16),
            pltpu.VMEM((width, width), BF16),
            pltpu.VMEM((width, tokens), BF16),
            pltpu.VMEM((tokens, 3 * width), BF16),
            pltpu.VMEM((tokens, width), BF16),
            pltpu.VMEM((width, tokens), BF16),
            pltpu.VMEM((tokens, 3 * width), BF16),
            pltpu.VMEM((patches, dates, width), BF16),
            pltpu.VMEM((chunks, spaces, 2, 2, rows, TILE), BF16),
            pltpu.VMEM((chunks, spaces, 2, rows, TILE), BF16),
            pltpu.VMEM((chunks, spaces, 2, rows, TILE), BF16),
            pltpu.VMEM((chunks, spaces, rows, TILE), BF16),
            pltpu.VMEM((chunks, spaces, rows, TILE), BF16),
            pltpu.VMEM((chunks, spaces - 1, rows, TILE), BF16),
            pltpu.VMEM((EARLY, spaces - 1, 2, rows, TILE), BF16),
            pltpu.VMEM((EARLY, 2, rows, TILE), BF16),
            pltpu.VMEM((EARLY, rows, TILE), BF16),
            dma((4,)),
            dma((groups, 3, 2)),
            dma((groups, 3, 2)),
            dma((groups, 3)),
            dma((groups, 3)),
            dma((chunks,)),
            dma((chunks,)),
            dma((chunks,)),
            dma((chunks,)),
            dma((chunks, spaces - 1)),
            dma((chunks, spaces - 1)),
        ],
        compiler_params=pltpu.CompilerParams(
            collective_id=0, has_side_effects=True, vmem_limit_bytes=56 * 2**20
        ),
    )(features.transpose(1, 0, 2), grad_out.transpose(1, 0, 2), w_qkv, w_out, valid_dates.T)
    return (gi.transpose(1, 0, 2), wg)


def local(features, grad_out, w_qkv, w_out, valid_dates):
    width = features.shape[-1]
    parts = 4 * lax.axis_size("space")
    tokens = valid_dates.size
    fits = (
        lax.axis_size("date") == 4
        and width % (16 * parts) == 0
        and features.shape[0] % 16 == 0
        and (4 * width // TILE) % (tokens // ROWS) == 0
        and 4 * width // TILE >= EARLY * (tokens // ROWS)
        and tokens >= 2 * ROWS
    )
    way = local_full if fits else local_plain
    return way(features, grad_out, w_qkv, w_out, valid_dates)


def solution(mesh):
    return jax.shard_map(
        local,
        mesh=mesh,
        in_specs=(
            P("date", ("groups", "space"), None),
            P("date", ("groups", "space"), None),
            P(),
            P(),
            P(None, ("groups", "space", "date")),
        ),
        out_specs=(P("date", ("groups", "space"), None), P(("groups", "space", "date"), None)),
        check_vma=False,
    )
```

```python
import jax
import jax.numpy as jnp
from jax import lax
from jax.experimental import pallas as pl
from jax.experimental.pallas import tpu as pltpu
from jax.sharding import PartitionSpec as P

HD = 64
epsilon = 1e-05
F32 = jnp.float32
BF16 = jnp.bfloat16
NT = (((1,), (1,)), ((), ()))
ROWS = 128


def stats(rows):
    flat = rows.astype(F32)
    centred = flat - jnp.mean(flat, axis=-1, keepdims=True)
    variance = jnp.mean(centred * centred, axis=-1, keepdims=True)
    inv_std = lax.rsqrt(variance + epsilon)
    return centred * inv_std, inv_std


def group_rows(ref, i):
    dates, width = ref.shape[1:]
    n = ROWS // dates
    return ref[pl.ds(i * n, n)].reshape(ROWS, width)


def project(i, f_ref, g_ref, wq_ref, wo_ref, nbt, qkv, da):
    normed, _ = stats(group_rows(f_ref, i))
    nb = normed.astype(BF16)
    at = pl.ds(pl.multiple_of(i * ROWS, ROWS), ROWS)
    nbt[:, at] = nb.T
    qkv[at, :] = jnp.dot(nb, wq_ref[...], preferred_element_type=F32).astype(BF16)
    da[at, :] = lax.dot_general(
        group_rows(g_ref, i), wo_ref[...], NT, preferred_element_type=F32
    ).astype(BF16)


def attend(i, dates, vd_ref, qkv, da, att, dqkv):
    width = da.shape[1]
    scale = 1.0 / HD**0.5
    at = pl.ds(pl.multiple_of(i * ROWS, ROWS), ROWS)
    n = ROWS // dates
    valid = vd_ref[...].astype(F32).T
    patch = lax.broadcasted_iota(jnp.int32, valid.shape, 1)
    valid = jnp.concatenate(
        [
            jnp.sum(jnp.where(patch == i * n + p, valid, 0.0), axis=1, keepdims=True)
            for p in range(n)
        ],
        axis=0,
    )
    row = lax.broadcasted_iota(jnp.int32, (ROWS, ROWS), 0)
    col = lax.broadcasted_iota(jnp.int32, (ROWS, ROWS), 1)
    keep = ((row // dates) == (col // dates)) & ((valid == 1.0) | (row == col))
    bias = jnp.where(keep, 0.0, -1e30).astype(F32)
    bias = jnp.concatenate([bias, bias], axis=1)
    lane = lax.broadcasted_iota(jnp.int32, (1, 2 * HD), 1)
    first = jnp.where(lane < HD, 1.0, 0.0)
    second = jnp.where(lane < HD, 0.0, 1.0)
    ones = (first.astype(BF16), second.astype(BF16))
    scales = ((first * scale).astype(BF16), (second * scale).astype(BF16))

    def stack(a, by):
        return jnp.concatenate([a * by[0], a * by[1]], axis=0)

    def halves(a):
        return jnp.concatenate([a[:HD, :ROWS], a[HD:, ROWS:]], axis=0).astype(BF16)

    for c in range(0, width, 2 * HD):
        q = stack(qkv[at, c : c + 2 * HD], scales)
        k = qkv[at, width + c : width + c + 2 * HD]
        v = qkv[at, 2 * width + c : 2 * width + c + 2 * HD]
        d = stack(da[at, c : c + 2 * HD], ones)
        s = lax.dot_general(k, q, NT, preferred_element_type=F32) + bias
        e = jnp.exp(s - jnp.max(s, axis=0, keepdims=True))
        prob = e * (1.0 / jnp.sum(e, axis=0, keepdims=True))
        prob_b = prob.astype(BF16)
        att[c : c + 2 * HD, at] = halves(jnp.dot(v.T, prob_b, preferred_element_type=F32))
        dp = lax.dot_general(v, d, NT, preferred_element_type=F32)
        delta = jnp.sum(prob * dp, axis=0, keepdims=True)
        ds = (prob * (dp - delta)).astype(BF16)
        k_scaled = k * jnp.asarray(scale, BF16)
        dqkv[at, c : c + 2 * HD] = halves(
            jnp.dot(k_scaled.T, ds, preferred_element_type=F32)
        ).T
        dqkv[at, width + c : width + c + 2 * HD] = jnp.dot(
            ds, q, preferred_element_type=F32
        ).astype(BF16)
        dqkv[at, 2 * width + c : 2 * width + c + 2 * HD] = jnp.dot(
            prob_b, d, preferred_element_type=F32
        ).astype(BF16)


def norm_backward(i, f_ref, g_ref, wq_ref, dqkv):
    at = pl.ds(pl.multiple_of(i * ROWS, ROWS), ROWS)
    dn = lax.dot_general(dqkv[at, :], wq_ref[...], NT, preferred_element_type=F32)
    normed, inv_std = stats(group_rows(f_ref, i))
    first = jnp.mean(dn, axis=-1, keepdims=True)
    second = jnp.mean(dn * normed, axis=-1, keepdims=True)
    return (group_rows(g_ref, i).astype(F32) + inv_std * (dn - first - normed * second)).astype(
        BF16
    )


def compute_kernel(f_ref, g_ref, wq_ref, wo_ref, vd_ref, gi_ref, wg_ref, nbt, qkv, da, att, dqkv):
    patches, dates, width = f_ref.shape
    groups = patches * dates // ROWS
    n = ROWS // dates

    @pl.loop(0, groups)
    def _(i):
        project(i, f_ref, g_ref, wq_ref, wo_ref, nbt, qkv, da)
        attend(i, dates, vd_ref, qkv, da, att, dqkv)
        gi_ref[pl.ds(i * n, n)] = norm_backward(i, f_ref, g_ref, wq_ref, dqkv).reshape(
            n, dates, width
        )

    tile = 256

    @pl.loop(0, 3 * width // tile)
    def _(j):
        at = pl.ds(pl.multiple_of(j * tile, tile), tile)
        wg_ref[:, at] = jnp.dot(nbt[...], dqkv[:, at], preferred_element_type=F32).astype(BF16)

    for j in range(0, width, tile):
        g = g_ref[:, :, j : j + tile].reshape(patches * dates, tile)
        wg_ref[:, 3 * width + j : 3 * width + j + tile] = jnp.dot(
            att[...], g, preferred_element_type=F32
        ).astype(BF16)


def local_plain(features, grad_out, w_qkv, w_out, valid_dates):
    width = features.shape[-1]
    dates, patches = valid_dates.shape
    tokens = dates * patches
    f = lax.all_to_all(features.transpose(1, 0, 2), "date", split_axis=0, concat_axis=1, tiled=True)
    g = lax.all_to_all(grad_out.transpose(1, 0, 2), "date", split_axis=0, concat_axis=1, tiled=True)
    vmem = pl.BlockSpec(memory_space=pltpu.VMEM)
    gi, wg = pl.pallas_call(
        compute_kernel,
        out_shape=(
            jax.ShapeDtypeStruct((patches, dates, width), BF16),
            jax.ShapeDtypeStruct((width, 4 * width), BF16),
        ),
        in_specs=[vmem] * 5,
        out_specs=(vmem, vmem),
        scratch_shapes=[
            pltpu.VMEM((width, tokens), BF16),
            pltpu.VMEM((tokens, 3 * width), BF16),
            pltpu.VMEM((tokens, width), BF16),
            pltpu.VMEM((width, tokens), BF16),
            pltpu.VMEM((tokens, 3 * width), BF16),
        ],
        compiler_params=pltpu.CompilerParams(vmem_limit_bytes=50 * 2**20),
    )(f, g, w_qkv, w_out, valid_dates.T)
    weight_grad = lax.psum_scatter(wg, ("space", "date"), scatter_dimension=0, tiled=True)
    grad_in = lax.all_to_all(gi, "date", split_axis=1, concat_axis=0, tiled=True)
    return (grad_in.transpose(1, 0, 2), weight_grad.astype(F32))


TILE = 256
LAG = 2
EARLY = 3
MESH = pl.DeviceIdType.MESH


def full_kernel(
    f_in, g_in, wq_in, wo_in, vd_ref, gi_out, wg_out,
    f_ref, g_ref, wq_ref, wo_ref, nbt, qkv, da, att, dqkv, gi, part, core_in, core_sum, x_in, x_sum, z_in, early_in, early_sum, last_in,
    load_sem, fs, fr, gs, gr, cs, cr, xs, xr, zs, zr,
):
    patches, dates, width = f_ref.shape
    near = f_in.shape[1]
    groups = patches * dates // ROWS
    n = ROWS // dates
    chunks = part.shape[0]
    spaces = x_sum.shape[1]
    inner = 3 * width // TILE
    date = lax.axis_index("date")
    space = lax.axis_index("space")
    core = lax.rem(date, 2)
    chip = date // 2
    peers = (date + 1 - 2 * core, lax.rem(date + 2, 4), 3 - date)

    def spaced(k):
        return lax.rem(space + k, spaces)

    barrier = pltpu.get_barrier_semaphore()
    for peer in peers:
        pl.semaphore_signal(barrier, inc=1, device_id={"date": peer}, device_id_type=MESH)
    for k in range(1, spaces):
        pl.semaphore_signal(barrier, inc=1, device_id={"space": spaced(k)}, device_id_type=MESH)

    here = pl.ds(pl.multiple_of(date * near, near), near)
    mine = pl.ds(date * patches, patches)
    loads = [
        pltpu.make_async_copy(f_in.at[mine], f_ref.at[:, here], load_sem.at[0]),
        pltpu.make_async_copy(g_in.at[mine], g_ref.at[:, here], load_sem.at[1]),
        pltpu.make_async_copy(wq_in, wq_ref, load_sem.at[2]),
        pltpu.make_async_copy(wo_in, wo_ref, load_sem.at[3]),
    ]
    for copy in loads:
        copy.start()
    pl.semaphore_wait(barrier, 2 + spaces)

    def forward(i, r, a):
        src, dst = ((f_in, f_ref), (g_in, g_ref))[a]
        return pltpu.make_async_remote_copy(
            src_ref=src.at[pl.ds(peers[r] * patches + i * n, n)],
            dst_ref=dst.at[pl.ds(i * n, n), here],
            send_sem=fs.at[i, r, a],
            recv_sem=fr.at[i, r, a],
            device_id={"date": peers[r]},
            device_id_type=MESH,
        )

    def backward(i, r):
        there = pl.ds(pl.multiple_of(peers[r] * near, near), near)
        return pltpu.make_async_remote_copy(
            src_ref=gi.at[pl.ds(i * n, n), there],
            dst_ref=gi_out.at[pl.ds(date * patches + i * n, n)],
            send_sem=gs.at[i, r],
            recv_sem=gr.at[i, r],
            device_id={"date": peers[r]},
            device_id_type=MESH,
        )

    def over_core(j):
        return pltpu.make_async_remote_copy(
            src_ref=part.at[j, :, :, 1 - core],
            dst_ref=core_in.at[j],
            send_sem=cs.at[j],
            recv_sem=cr.at[j],
            device_id={"date": peers[0]},
            device_id_type=MESH,
        )

    def over_chip(j):
        return pltpu.make_async_remote_copy(
            src_ref=core_sum.at[j, :, 1 - chip],
            dst_ref=x_in.at[j],
            send_sem=xs.at[j],
            recv_sem=xr.at[j],
            device_id={"date": peers[1]},
            device_id_type=MESH,
        )

    def over_space(j, k):
        return pltpu.make_async_remote_copy(
            src_ref=x_sum.at[j, spaced(k)],
            dst_ref=z_in.at[j, k - 1],
            send_sem=zs.at[j, k - 1],
            recv_sem=zr.at[j, k - 1],
            device_id={"space": spaced(k)},
            device_id_type=MESH,
        )

    def early_space(j, k):
        return pltpu.make_async_remote_copy(
            src_ref=core_sum.at[j, spaced(k)],
            dst_ref=early_in.at[j, k - 1],
            send_sem=zs.at[j, k - 1],
            recv_sem=zr.at[j, k - 1],
            device_id={"space": spaced(k)},
            device_id_type=MESH,
        )

    def late_chip(j):
        return pltpu.make_async_remote_copy(
            src_ref=early_sum.at[j, 1 - chip],
            dst_ref=last_in.at[j],
            send_sem=xs.at[j],
            recv_sem=xr.at[j],
            device_id={"date": peers[1]},
            device_id_type=MESH,
        )

    @pl.loop(0, groups)
    def _(i):
        for r in (1, 2, 0):
            for a in range(2):
                forward(i, r, a).start()

    for copy in loads:
        copy.wait()

    @pl.loop(0, groups)
    def _(i):
        for r in range(3):
            for a in range(2):
                forward(i, r, a).wait_recv()
        project(i, f_ref, g_ref, wq_ref, wo_ref, nbt, qkv, da)
        attend(i, dates, vd_ref, qkv, da, att, dqkv)

    @pl.loop(0, chunks + LAG)
    def _(j):
        @pl.when(j < inner)
        def _():
            at = pl.ds(pl.multiple_of(j * TILE, TILE), TILE)
            w = jnp.dot(nbt[...], dqkv[:, at], preferred_element_type=F32).astype(BF16)
            part[j] = w.reshape(part.shape[1:])

        @pl.when((j >= inner) & (j < chunks))
        def _():
            at = pl.ds(pl.multiple_of((j - inner) * TILE, TILE), TILE)
            g = g_ref[:, :, at].reshape(patches * dates, TILE)
            w = jnp.dot(att[...], g, preferred_element_type=F32).astype(BF16)
            part[j] = w.reshape(part.shape[1:])

        @pl.when(j < chunks)
        def _():
            over_core(j).start()

        @pl.when(j >= LAG)
        def _():
            b = j - LAG
            over_core(b).wait_recv()
            total = part[b, :, :, core].astype(F32) + core_in[b].astype(F32)
            core_sum[b] = total.astype(BF16)

            @pl.when(b < EARLY)
            def _():
                for k in range(1, spaces):
                    early_space(b, k).start()

            @pl.when(b >= EARLY)
            def _():
                over_chip(b).start()

    share = chunks // groups

    @pl.loop(0, groups)
    def _(i):
        gi[pl.ds(i * n, n)] = norm_backward(i, f_ref, g_ref, wq_ref, dqkv).reshape(n, dates, width)
        for r in (1, 2, 0):
            backward(i, r).start()

        @pl.when(i == 2)
        def _():
            @pl.loop(0, EARLY)
            def _(j):
                total = core_sum[j, space].astype(F32)
                for k in range(1, spaces):
                    early_space(j, k).wait_recv()
                    total += early_in[j, k - 1].astype(F32)
                early_sum[j] = total.astype(BF16)
                late_chip(j).start()

        @pl.loop(i * share, (i + 1) * share)
        def _(j):
            @pl.when(j >= EARLY)
            def _():
                over_chip(j).wait_recv()
                total = core_sum[j, :, chip].astype(F32) + x_in[j].astype(F32)
                x_sum[j] = total.astype(BF16)
                for k in range(1, spaces):
                    over_space(j, k).start()

    own = pltpu.make_async_copy(gi.at[:, here], gi_out.at[mine], load_sem.at[0])
    own.start()

    @pl.loop(EARLY, chunks)
    def _(j):
        total = x_sum[j, space].astype(F32)
        for k in range(1, spaces):
            over_space(j, k).wait_recv()
            total += z_in[j, k - 1].astype(F32)
        wg_out[:, pl.ds(pl.multiple_of(j * TILE, TILE), TILE)] = total
        over_core(j).wait_send()
        over_chip(j).wait_send()
        for k in range(1, spaces):
            over_space(j, k).wait_send()

    @pl.loop(0, EARLY)
    def _(j):
        late_chip(j).wait_recv()
        total = early_sum[j, chip].astype(F32) + last_in[j].astype(F32)
        wg_out[:, pl.ds(pl.multiple_of(j * TILE, TILE), TILE)] = total
        over_core(j).wait_send()
        late_chip(j).wait_send()
        for k in range(1, spaces):
            early_space(j, k).wait_send()

    own.wait()

    @pl.loop(0, groups)
    def _(i):
        for r in range(3):
            backward(i, r).wait()
            for a in range(2):
                forward(i, r, a).wait_send()


def local_full(features, grad_out, w_qkv, w_out, valid_dates):
    width = features.shape[-1]
    dates, patches = valid_dates.shape
    near, wide = features.shape[:2]
    tokens = dates * patches
    groups = tokens // ROWS
    spaces = lax.axis_size("space")
    chunks = 4 * width // TILE
    rows = width // (4 * spaces)
    vmem = pl.BlockSpec(memory_space=pltpu.VMEM)
    anywhere = pl.BlockSpec(memory_space=pl.ANY)
    dma = pltpu.SemaphoreType.DMA
    gi, wg = pl.pallas_call(
        full_kernel,
        out_shape=(
            jax.ShapeDtypeStruct((wide, near, width), BF16),
            jax.ShapeDtypeStruct((rows, 4 * width), F32),
        ),
        in_specs=[anywhere] * 4 + [vmem],
        out_specs=(anywhere, vmem),
        scratch_shapes=[
            pltpu.VMEM((patches, dates, width), BF16),
            pltpu.VMEM((patches, dates, width), BF16),
            pltpu.VMEM((width, 3 * width), BF16),
            pltpu.VMEM((width, width), BF16),
            pltpu.VMEM((width, tokens), BF16),
            pltpu.VMEM((tokens, 3 * width), BF16),
            pltpu.VMEM((tokens, width), BF16),
            pltpu.VMEM((width, tokens), BF16),
            pltpu.VMEM((tokens, 3 * width), BF16),
            pltpu.VMEM((patches, dates, width), BF16),
            pltpu.VMEM((chunks, spaces, 2, 2, rows, TILE), BF16),
            pltpu.VMEM((chunks, spaces, 2, rows, TILE), BF16),
            pltpu.VMEM((chunks, spaces, 2, rows, TILE), BF16),
            pltpu.VMEM((chunks, spaces, rows, TILE), BF16),
            pltpu.VMEM((chunks, spaces, rows, TILE), BF16),
            pltpu.VMEM((chunks, spaces - 1, rows, TILE), BF16),
            pltpu.VMEM((EARLY, spaces - 1, 2, rows, TILE), BF16),
            pltpu.VMEM((EARLY, 2, rows, TILE), BF16),
            pltpu.VMEM((EARLY, rows, TILE), BF16),
            dma((4,)),
            dma((groups, 3, 2)),
            dma((groups, 3, 2)),
            dma((groups, 3)),
            dma((groups, 3)),
            dma((chunks,)),
            dma((chunks,)),
            dma((chunks,)),
            dma((chunks,)),
            dma((chunks, spaces - 1)),
            dma((chunks, spaces - 1)),
        ],
        compiler_params=pltpu.CompilerParams(
            collective_id=0, has_side_effects=True, vmem_limit_bytes=56 * 2**20
        ),
    )(features.transpose(1, 0, 2), grad_out.transpose(1, 0, 2), w_qkv, w_out, valid_dates.T)
    return (gi.transpose(1, 0, 2), wg)


def local(features, grad_out, w_qkv, w_out, valid_dates):
    width = features.shape[-1]
    parts = 4 * lax.axis_size("space")
    tokens = valid_dates.size
    fits = (
        lax.axis_size("date") == 4
        and width % (16 * parts) == 0
        and features.shape[0] % 16 == 0
        and (4 * width // TILE) % (tokens // ROWS) == 0
        and 4 * width // TILE >= EARLY * (tokens // ROWS)
        and tokens >= 3 * ROWS
    )
    way = local_full if fits else local_plain
    return way(features, grad_out, w_qkv, w_out, valid_dates)


def solution(mesh):
    return jax.shard_map(
        local,
        mesh=mesh,
        in_specs=(
            P("date", ("groups", "space"), None),
            P("date", ("groups", "space"), None),
            P(),
            P(),
            P(None, ("groups", "space", "date")),
        ),
        out_specs=(P("date", ("groups", "space"), None), P(("groups", "space", "date"), None)),
        check_vma=False,
    )
```
